128 devices in a mesh: grp: 4 (over x), wide: 32 (over y, z, core).
Axes of the slice: x: 4, y: 4, z: 4, core: 2. Of those that a mesh axis runs over, the one named last changes fastest.
Arguments:
- fine_pop: float32 [256, 19, 4096], P(('grp', 'wide')), may hold values from 0 to 1, as said below
- coarse_pop: float32 [19, 32, 8, 4096], P(None, 'grp', None, 'wide'), may hold values from 0 to 1, as said below
- new_slot: int32 [256], replicated, may hold values from 0 to 255, each once
Outputs:
- fine_out: float32 [256, 19, 4096], P(('grp', 'wide'))
- coarse_out: float32 [19, 32, 8, 4096], P(None, 'grp', None, 'wide')
The draws below stay inside these ranges and needn't reach their ends.
Inputs may be any that keep to these rules, and one draw needn't show every extreme that they name: A permutation: fine block b moves to slot new_slot[b]. `fine_pop`: positive populations near equilibrium, densities of order one, speeds under 0.25. `coarse_pop`: positive populations near equilibrium, densities of order one, speeds under 0.25.
All inputs are finite; a program needn't handle non-finite values.
Results may differ from the reference program's by a relative error of at most 0.00002.
Values sent between devices are 32-bit elements; how exact they have to be, the bound alone decides.
A program may use at most 128 MiB of HBM per device.

```python
import jax
import jax.numpy as jnp
from jax import lax

B = 16
FB_DEV = 2
CY = 128
FINE_BLOCKS = 256
COARSE_X = 32
COARSE_Y = 4096
N_GRP = 4
N_WIDE = 32


VELOCITIES = ((0, 0, 0), (1, 0, 0), (-1, 0, 0), (0, 1, 0), (0, -1, 0), (0, 0, 1), (0, 0, -1), (1, 1, 0), (-1, -1, 0), (1, -1, 0), (-1, 1, 0), (1, 0, 1), (-1, 0, -1), (1, 0, -1), (-1, 0, 1), (0, 1, 1), (0, -1, -1), (0, 1, -1), (0, -1, 1))


WEIGHTS = (1.0 / 3.0,) + (1.0 / 18.0,) * 6 + (1.0 / 36.0,) * 12


def draw_state(key, leading, cell_count):
    subkeys = jax.random.split(key, 5)
    density = jax.random.uniform(subkeys[1], (leading, cell_count), jnp.float32, minval=0.5, maxval=1.5)
    motion = jnp.zeros((leading, 3, 1), jnp.float32)
    velocity = jnp.clip(0.04 * jax.random.normal(subkeys[2], (leading, 3, cell_count), jnp.float32) + motion, -0.12, 0.12)
    jitter = jnp.clip(0.1 * jax.random.normal(subkeys[3], (leading, 19, cell_count), jnp.float32), -0.3, 0.3)
    squared = velocity[:, 0] * velocity[:, 0] + velocity[:, 1] * velocity[:, 1] + velocity[:, 2] * velocity[:, 2]
    entries = []
    for direction in range(19):
        offset = VELOCITIES[direction]
        projected = offset[0] * velocity[:, 0] + offset[1] * velocity[:, 1] + offset[2] * velocity[:, 2]
        entries.append(WEIGHTS[direction] * density * (1.0 + 3.0 * projected + 4.5 * projected * projected - 1.5 * squared))
    return jnp.stack(entries, axis=1) * (1.0 + jitter)


def draw_fine_pop(key, part):
    return draw_state(key, FINE_BLOCKS, B ** 3)


def draw_coarse_pop(key, part):
    values = draw_state(key, COARSE_X, B // 2 * COARSE_Y)
    return values.transpose(1, 0, 2).reshape(19, COARSE_X, B // 2, COARSE_Y)


def setup_inputs(seed: int = 0) -> dict:
    keys = jax.random.split(jax.random.key(seed), 4)
    fine_pop = draw_fine_pop(jax.random.fold_in(keys[3], 71), 0)
    coarse_pop = draw_coarse_pop(jax.random.fold_in(keys[3], 71), 0)
    new_slot = jax.random.permutation(keys[2], FINE_BLOCKS).astype(jnp.int32)
    return dict(fine_pop=fine_pop, coarse_pop=coarse_pop, new_slot=new_slot)


VELOCITIES = ((0, 0, 0), (1, 0, 0), (-1, 0, 0), (0, 1, 0), (0, -1, 0), (0, 0, 1), (0, 0, -1),
              (1, 1, 0), (-1, -1, 0), (1, -1, 0), (-1, 1, 0), (1, 0, 1), (-1, 0, -1), (1, 0, -1),
              (-1, 0, 1), (0, 1, 1), (0, -1, -1), (0, 1, -1), (0, -1, 1))
WEIGHTS = (1.0 / 3.0,) + (1.0 / 18.0,) * 6 + (1.0 / 36.0,) * 12
COUPLING = -5.0
FINE_TAU = 1.1
COARSE_TAU = 0.8
TO_COARSE = 2.0 * COARSE_TAU / FINE_TAU
TO_FINE = FINE_TAU / (2.0 * COARSE_TAU)


def moments(state):
    density = state[0]
    momentum = [jnp.zeros_like(state[0]), jnp.zeros_like(state[0]), jnp.zeros_like(state[0])]
    for direction in range(1, 19):
        offset = VELOCITIES[direction]
        density = density + state[direction]
        for component in range(3):
            if offset[component] != 0:
                momentum[component] = momentum[component] + offset[component] * state[direction]
    return density, momentum


def equilibrium(density, velocity):
    squared = velocity[0] * velocity[0] + velocity[1] * velocity[1] + velocity[2] * velocity[2]
    entries = []
    for direction in range(19):
        offset = VELOCITIES[direction]
        projected = jnp.zeros_like(density)
        for component in range(3):
            if offset[component] != 0:
                projected = projected + offset[component] * velocity[component]
        entries.append(WEIGHTS[direction] * density * (1.0 + 3.0 * projected + 4.5 * projected * projected - 1.5 * squared))
    return jnp.stack(entries)


def rescale(state, factor):
    density, momentum = moments(state)
    velocity = []
    for component in range(3):
        velocity.append(momentum[component] / density)
    balance = equilibrium(density, velocity)
    return balance + factor * (state - balance)


def restrict(layers):
    extent_x = layers.shape[1]
    extent_z = layers.shape[2]
    grouped = layers.reshape(layers.shape[0], extent_x // 2, 2, extent_z // 2, 2, 2)
    return 0.125 * jnp.sum(grouped, axis=(2, 4, 5))


def upsample(boundary):
    return jnp.repeat(jnp.repeat(boundary, 2, axis=-2), 2, axis=-1)


def window(padded, shift_x, shift_y, shift_z):
    extent_x = padded.shape[-3] - 2
    extent_z = padded.shape[-2] - 2
    extent_y = padded.shape[-1] - 2
    return padded[..., 1 + shift_x:1 + shift_x + extent_x, 1 + shift_z:1 + shift_z + extent_z, 1 + shift_y:1 + shift_y + extent_y]


def collide(state, density, momentum, potential, padded_potential, relaxation):
    gradient = [jnp.zeros_like(density), jnp.zeros_like(density), jnp.zeros_like(density)]
    for direction in range(1, 19):
        offset = VELOCITIES[direction]
        neighbor = window(padded_potential, offset[0], offset[1], offset[2])
        for component in range(3):
            if offset[component] != 0:
                gradient[component] = gradient[component] + (WEIGHTS[direction] * offset[component]) * neighbor
    velocity = []
    for component in range(3):
        velocity.append((momentum[component] - relaxation * COUPLING * potential * gradient[component]) / density)
    balance = equilibrium(density, velocity)
    return state + (balance - state) / relaxation


def propagate(padded_post):
    entries = []
    for direction in range(19):
        offset = VELOCITIES[direction]
        entries.append(window(padded_post[direction], -offset[0], -offset[1], -offset[2]))
    return jnp.stack(entries)


def lattice_step(state, relaxation, ghosts):
    potential_low, potential_high, post_low, post_high = ghosts
    density, momentum = moments(state)
    potential = 1.0 - jnp.exp(-density)
    padded_potential = pad_slab(potential[None], potential_low[None], potential_high[None])[0]
    post = collide(state, density, momentum, potential, padded_potential, relaxation)
    return propagate(pad_slab(post, post_low, post_high))


def coarse_ghosts(restricted):
    density, momentum = moments(restricted)
    return 1.0 - jnp.exp(-density), rescale(restricted, TO_COARSE)


def fine_ghosts(boundary):
    density, momentum = moments(boundary)
    return upsample(1.0 - jnp.exp(-density)), upsample(rescale(boundary, TO_FINE))


def pad_slab(state, ghost_low, ghost_high):
    with_rows = jnp.concatenate([ghost_low[..., None], state, ghost_high[..., None]], axis=3)
    with_sides = jnp.concatenate([with_rows[:, -1:], with_rows, with_rows[:, :1]], axis=1)
    return jnp.concatenate([with_sides[:, :, -1:], with_sides, with_sides[:, :, :1]], axis=2)


def slab_update(items):
    fine_slab, coarse_slab, next_first, previous_last = items
    low_potential, low_post = coarse_ghosts(restrict(fine_slab[..., -2:]))
    high_potential, high_post = coarse_ghosts(restrict(next_first))
    coarse_new = lattice_step(coarse_slab, COARSE_TAU, (low_potential, high_potential, low_post, high_post))
    fine_low_potential, fine_low_post = fine_ghosts(previous_last)
    fine_high_potential, fine_high_post = fine_ghosts(coarse_slab[..., 0])
    ghosts = (fine_low_potential, fine_high_potential, fine_low_post, fine_high_post)
    for substep in range(2):
        fine_slab = lattice_step(fine_slab, FINE_TAU, ghosts)
    return fine_slab, coarse_new


def reference(fine_pop, coarse_pop, new_slot):
    block_count = new_slot.shape[0]
    inverse = jnp.zeros((block_count,), jnp.int32).at[new_slot].set(jnp.arange(block_count, dtype=jnp.int32))
    arranged = fine_pop[inverse]
    fine_slabs = arranged.reshape(N_GRP, N_WIDE, FB_DEV, 19, B, B, B).transpose(1, 3, 0, 4, 5, 2, 6)
    fine_slabs = fine_slabs.reshape(N_WIDE, 19, N_GRP * B, B, FB_DEV * B)
    coarse_slabs = coarse_pop.reshape(19, COARSE_X, B // 2, N_WIDE, CY).transpose(3, 0, 1, 2, 4)
    next_first = jnp.roll(fine_slabs[..., :2], -1, axis=0)
    previous_last = jnp.roll(coarse_slabs[..., -1], 1, axis=0)
    fine_new, coarse_new = lax.map(slab_update, (fine_slabs, coarse_slabs, next_first, previous_last))
    fine_out = fine_new.reshape(N_WIDE, 19, N_GRP, B, B, FB_DEV, B).transpose(2, 0, 5, 1, 3, 4, 6)
    fine_out = fine_out.reshape(block_count, 19, B ** 3)
    coarse_out = coarse_new.transpose(1, 2, 3, 0, 4).reshape(19, COARSE_X, B // 2, N_WIDE * CY)
    return fine_out, coarse_out
```

```python
import functools

import jax
import jax.numpy as jnp
from jax import lax
from jax.experimental import pallas as pl
from jax.experimental.pallas import tpu as pltpu
from jax.sharding import PartitionSpec as P

B = 16
LOGICAL = pl.DeviceIdType.MESH


VELOCITIES = (
    (0, 0, 0),
    (1, 0, 0),
    (-1, 0, 0),
    (0, 1, 0),
    (0, -1, 0),
    (0, 0, 1),
    (0, 0, -1),
    (1, 1, 0),
    (-1, -1, 0),
    (1, -1, 0),
    (-1, 1, 0),
    (1, 0, 1),
    (-1, 0, -1),
    (1, 0, -1),
    (-1, 0, 1),
    (0, 1, 1),
    (0, -1, -1),
    (0, 1, -1),
    (0, -1, 1),
)
WEIGHTS = (1.0 / 3.0,) + (1.0 / 18.0,) * 6 + (1.0 / 36.0,) * 12
COUPLING = -5.0
FINE_TAU = 1.1
COARSE_TAU = 0.8
TO_COARSE = 2.0 * COARSE_TAU / FINE_TAU
TO_FINE = FINE_TAU / (2.0 * COARSE_TAU)


def extended(cells, sides, width):
    for axis, dim in sides:
        count = lax.axis_size(axis)
        head = lax.slice_in_dim(cells, 0, width, axis=dim)
        tail = lax.slice_in_dim(cells, cells.shape[dim] - width, cells.shape[dim], axis=dim)
        cells = jnp.concatenate(
            [
                lax.ppermute(tail, axis, [(i, (i + 1) % count) for i in range(count)]),
                cells,
                lax.ppermute(head, axis, [((i + 1) % count, i) for i in range(count)]),
            ],
            axis=dim,
        )
    return cells


def moments(state):
    density = state[0]
    momentum = [jnp.zeros_like(state[0]), jnp.zeros_like(state[0]), jnp.zeros_like(state[0])]
    for direction in range(1, 19):
        offset = VELOCITIES[direction]
        density = density + state[direction]
        for component in range(3):
            if offset[component] != 0:
                momentum[component] = momentum[component] + offset[component] * state[direction]
    return (density, momentum)


def equilibrium(density, velocity):
    squared = velocity[0] * velocity[0] + velocity[1] * velocity[1] + velocity[2] * velocity[2]
    entries = []
    for direction in range(19):
        offset = VELOCITIES[direction]
        projected = jnp.zeros_like(density)
        for component in range(3):
            if offset[component] != 0:
                projected = projected + offset[component] * velocity[component]
        entries.append(
            WEIGHTS[direction]
            * density
            * (1.0 + 3.0 * projected + 4.5 * projected * projected - 1.5 * squared)
        )
    return jnp.stack(entries)


def rescale(state, factor):
    density, momentum = moments(state)
    velocity = []
    for component in range(3):
        velocity.append(momentum[component] / density)
    balance = equilibrium(density, velocity)
    return balance + factor * (state - balance)


def restrict(layers):
    extent_x = layers.shape[1]
    extent_z = layers.shape[2]
    grouped = layers.reshape(layers.shape[0], extent_x // 2, 2, extent_z // 2, 2, 2)
    return 0.125 * jnp.sum(grouped, axis=(2, 4, 5))


def upsample(boundary):
    return jnp.repeat(jnp.repeat(boundary, 2, axis=-2), 2, axis=-1)


def window(padded, shift_x, shift_y, shift_z):
    extent_x = padded.shape[-3] - 2
    extent_z = padded.shape[-2] - 2
    extent_y = padded.shape[-1] - 2
    return padded[
        ...,
        1 + shift_x : 1 + shift_x + extent_x,
        1 + shift_z : 1 + shift_z + extent_z,
        1 + shift_y : 1 + shift_y + extent_y,
    ]


def collide(state, density, momentum, potential, padded_potential, relaxation):
    gradient = [jnp.zeros_like(density), jnp.zeros_like(density), jnp.zeros_like(density)]
    for direction in range(1, 19):
        offset = VELOCITIES[direction]
        neighbor = window(padded_potential, offset[0], offset[1], offset[2])
        for component in range(3):
            if offset[component] != 0:
                gradient[component] = (
                    gradient[component] + WEIGHTS[direction] * offset[component] * neighbor
                )
    velocity = []
    for component in range(3):
        velocity.append(
            (momentum[component] - relaxation * COUPLING * potential * gradient[component])
            / density
        )
    balance = equilibrium(density, velocity)
    return state + (balance - state) / relaxation


def propagate(padded_post):
    entries = []
    for direction in range(19):
        offset = VELOCITIES[direction]
        entries.append(window(padded_post[direction], -offset[0], -offset[1], -offset[2]))
    return jnp.stack(entries)


def extend(state, ghost_low, ghost_high):
    with_rows = jnp.concatenate([ghost_low[..., None], state, ghost_high[..., None]], axis=3)
    with_sides = extended(with_rows, (("grp", 1),), 1)
    return jnp.concatenate([with_sides[:, :, -1:], with_sides, with_sides[:, :, :1]], axis=2)


def lattice_step(state, relaxation, ghosts):
    potential_low, potential_high, post_low, post_high = ghosts
    density, momentum = moments(state)
    potential = 1.0 - jnp.exp(-density)
    padded_potential = extend(potential[None], potential_low[None], potential_high[None])[0]
    post = collide(state, density, momentum, potential, padded_potential, relaxation)
    return propagate(extend(post, post_low, post_high))


def coarse_ghosts(restricted):
    density, momentum = moments(restricted)
    return (1.0 - jnp.exp(-density), rescale(restricted, TO_COARSE))


def fine_ghosts(boundary):
    density, momentum = moments(boundary)
    return (upsample(1.0 - jnp.exp(-density)), upsample(rescale(boundary, TO_FINE)))


OFFSETS = sorted(
    ((a, b, c, d) for a in range(4) for b in range(4) for c in range(4) for d in range(2) if a + b + c + d),
    key=lambda o: (-sum(min(v, 4 - v) for v in o[:3]), (o[0] * 7 + o[1] * 5 + o[2] * 3 + o[3]) % 11),
)


def device_of(offset):
    g, w = lax.axis_index("grp"), lax.axis_index("wide")
    x = lax.rem(g + offset[0], 4)
    y = lax.rem(w // 8 + offset[1], 4)
    z = lax.rem(lax.rem(w // 2, 4) + offset[2], 4)
    c = lax.rem(lax.rem(w, 2) + offset[3], 2)
    return x, (y * 4 + z) * 2 + c


def migrate_kernel(fine, slots, out, p1, r1, p2, r2, inv_v, inv_s, s1, q1, s2, q2, s3):
    me = lax.axis_index("grp") * 32 + lax.axis_index("wide")
    barrier = pltpu.get_barrier_semaphore()
    for offset in OFFSETS:
        pl.semaphore_signal(barrier, inc=1, device_id=device_of(offset), device_id_type=LOGICAL)

    def pack(t, _):
        for k in range(2):
            v = fine[k, :, pl.ds(pl.multiple_of(t * 128, 128), 128)]
            for q in range(4):
                rows = min(5, 19 - 5 * q)
                p1[k, t * 4 + q, 0:rows, :] = v[5 * q : 5 * q + rows]
        return 0

    lax.fori_loop(0, 32, pack, 0)

    place = lax.broadcasted_iota(jnp.int32, (8, 128), 0) * 128 + lax.broadcasted_iota(jnp.int32, (8, 128), 1)

    def invert(b, acc):
        return jnp.where(place == slots[b], b, acc)

    inv_v[...] = lax.fori_loop(0, 256, invert, jnp.zeros((8, 128), jnp.int32))
    fetch = pltpu.make_async_copy(inv_v, inv_s, s3)
    fetch.start()
    for k in range(2):
        r1[2 * me + k, 0:5, :] = p1[k, me, 0:5, :]
    pl.semaphore_wait(barrier, len(OFFSETS))
    for offset in OFFSETS:
        x, w = device_of(offset)
        pltpu.make_async_remote_copy(
            src_ref=p1.at[:, x * 32 + w, 0:5, :],
            dst_ref=r1.at[pl.ds(2 * me, 2), 0:5, :],
            send_sem=s1,
            recv_sem=q1,
            device_id=(x, w),
            device_id_type=LOGICAL,
        ).start()
    fetch.wait()
    all1 = r1.at[0:254, 0:5, :]
    pltpu.make_async_copy(all1, all1, q1).wait()

    def permute(m, _):
        for k in range(2):
            s = 2 * m + k
            p2[k, m, 0:5, :] = r1[inv_s[s // 128, lax.rem(s, 128)], 0:5, :]
        return 0

    lax.fori_loop(0, 128, permute, 0)
    for k in range(2):
        r2[k, me, 0:5, :] = p2[k, me, 0:5, :]
    for offset in OFFSETS:
        x, w = device_of(offset)
        pltpu.make_async_remote_copy(
            src_ref=p2.at[:, x * 32 + w, 0:5, :],
            dst_ref=r2.at[:, me, 0:5, :],
            send_sem=s2,
            recv_sem=q2,
            device_id=(x, w),
            device_id_type=LOGICAL,
        ).start()
    all2 = r2.at[:, 0:127, 0:5, :]
    pltpu.make_async_copy(all2, all2, q2).wait()
    pltpu.make_async_copy(all1, all1, s1).wait()
    pltpu.make_async_copy(all2, all2, s2).wait()
    out[:, :, 0:5, :] = r2[:, :, 0:5, :]


def migrate(fine_pop, new_slot):
    pieces = (2, 128, 8, 128)
    got = pl.pallas_call(
        migrate_kernel,
        out_shape=jax.ShapeDtypeStruct(pieces, jnp.float32),
        in_specs=[pl.BlockSpec(memory_space=pltpu.VMEM), pl.BlockSpec(memory_space=pltpu.SMEM)],
        out_specs=pl.BlockSpec(memory_space=pltpu.VMEM),
        scratch_shapes=[
            pltpu.VMEM(pieces, jnp.float32),
            pltpu.VMEM((256, 8, 128), jnp.float32),
            pltpu.VMEM(pieces, jnp.float32),
            pltpu.VMEM(pieces, jnp.float32),
            pltpu.VMEM((8, 128), jnp.int32),
            pltpu.SMEM((8, 128), jnp.int32),
        ]
        + [pltpu.SemaphoreType.DMA] * 5,
        compiler_params=pltpu.CompilerParams(
            collective_id=0, has_side_effects=True, vmem_limit_bytes=48 * 2**20
        ),
    )(fine_pop, new_slot)
    got = got[:, :, :5].reshape(2, 32, 20, 128)[:, :, :19]
    return got.transpose(0, 2, 1, 3).reshape(2, 19, 4096)

def local(fine_pop, coarse_pop, new_slot):
    local_blocks = fine_pop.shape[0]
    own_blocks = migrate(fine_pop, new_slot)
    fine_grid = (
        own_blocks.reshape(local_blocks, 19, B, B, B)
        .transpose(1, 2, 3, 0, 4)
        .reshape(19, B, B, local_blocks * B)
    )
    lower_item = restrict(fine_grid[..., :2])
    upper_item = coarse_pop[..., -1]
    bundle = jnp.stack([lower_item, upper_item], axis=3)
    received = extended(bundle, (("wide", 3),), 1)
    low_potential, low_post = coarse_ghosts(restrict(fine_grid[..., -2:]))
    high_potential, high_post = coarse_ghosts(received[..., 3])
    coarse_out = lattice_step(
        coarse_pop, COARSE_TAU, (low_potential, high_potential, low_post, high_post)
    )
    fine_low_potential, fine_low_post = fine_ghosts(received[..., 0])
    fine_high_potential, fine_high_post = fine_ghosts(coarse_pop[..., 0])
    ghosts = (fine_low_potential, fine_high_potential, fine_low_post, fine_high_post)
    for substep in range(2):
        fine_grid = lattice_step(fine_grid, FINE_TAU, ghosts)
    fine_out = (
        fine_grid.reshape(19, B, B, local_blocks, B)
        .transpose(3, 0, 1, 2, 4)
        .reshape(local_blocks, 19, B**3)
    )
    return (fine_out, coarse_out)


def solution(mesh):
    return jax.shard_map(
        local,
        mesh=mesh,
        in_specs=(P(("grp", "wide"), None, None), P(None, "grp", None, "wide"), P()),
        out_specs=(P(("grp", "wide"), None, None), P(None, "grp", None, "wide")),
        check_vma=False,
    )
```

```python
import jax
import jax.numpy as jnp
from jax import lax
from jax.experimental import pallas as pl
from jax.experimental.pallas import tpu as pltpu
from jax.sharding import PartitionSpec as P

VELOCITIES = (
    (0, 0, 0),
    (1, 0, 0),
    (-1, 0, 0),
    (0, 1, 0),
    (0, -1, 0),
    (0, 0, 1),
    (0, 0, -1),
    (1, 1, 0),
    (-1, -1, 0),
    (1, -1, 0),
    (-1, 1, 0),
    (1, 0, 1),
    (-1, 0, -1),
    (1, 0, -1),
    (-1, 0, 1),
    (0, 1, 1),
    (0, -1, -1),
    (0, 1, -1),
    (0, -1, 1),
)
WEIGHTS = (1.0 / 3.0,) + (1.0 / 18.0,) * 6 + (1.0 / 36.0,) * 12
COUPLING = -5.0
FINE_TAU = 1.1
COARSE_TAU = 0.8
TO_COARSE = 2.0 * COARSE_TAU / FINE_TAU
TO_FINE = FINE_TAU / (2.0 * COARSE_TAU)

INDEX = {c: i for i, c in enumerate(VELOCITIES)}
X_PLUS = (1, 7, 9, 11, 13)
X_MINUS = tuple(INDEX[(-c[0], c[1], c[2])] for c in (VELOCITIES[i] for i in X_PLUS))
Y_PLUS = (3, 7, 10, 15, 17)
Y_MINUS = tuple(INDEX[(c[0], -c[1], c[2])] for c in (VELOCITIES[i] for i in Y_PLUS))

OFFSETS = sorted(
    ((a, b, c, d) for a in range(4) for b in range(4) for c in range(4) for d in range(2) if a + b + c + d),
    key=lambda o: (-sum(min(v, 4 - v) for v in o[:3]), (o[0] * 7 + o[1] * 5 + o[2] * 3 + o[3]) % 11),
)


def send(src, dst, sems, device):
    return pltpu.make_async_remote_copy(
        src_ref=src,
        dst_ref=dst,
        send_sem=sems.at[0],
        recv_sem=sems.at[1],
        device_id=device,
        device_id_type=pl.DeviceIdType.MESH,
    )


def device_of(offset):
    g, w = lax.axis_index("grp"), lax.axis_index("wide")
    x = lax.rem(g + offset[0], 4)
    y = lax.rem(w // 8 + offset[1], 4)
    z = lax.rem(lax.rem(w // 2, 4) + offset[2], 4)
    c = lax.rem(lax.rem(w, 2) + offset[3], 2)
    return x, (y * 4 + z) * 2 + c


def lane():
    return lax.broadcasted_iota(jnp.int32, (8, 128), 1)


def sub():
    return lax.broadcasted_iota(jnp.int32, (8, 128), 0)


def rot(v, shift):
    return pltpu.roll(v, shift % 128, 1)


def turn(v, shift):
    return pltpu.roll(v, shift % 8, 0)


def potential(density):
    return 1.0 - jnp.exp(-density)


def moments(state):
    density = state[0]
    momentum = [None, None, None]
    for d in range(1, 19):
        density = density + state[d]
        for a in range(3):
            c = VELOCITIES[d][a]
            if c:
                m = momentum[a]
                momentum[a] = c * state[d] if m is None else (m + state[d] if c > 0 else m - state[d])
    return [density] + momentum


def relax(density, velocity, states, keep, gain):
    base = 1.0 - 1.5 * (velocity[0] * velocity[0] + velocity[1] * velocity[1] + velocity[2] * velocity[2])
    scaled = {w: (gain * w) * density for w in set(WEIGHTS[d] for d, _ in states)}
    entries = []
    for d, h in states:
        along = None
        for a in range(3):
            c = VELOCITIES[d][a]
            if c:
                term = velocity[a] if c > 0 else -velocity[a]
                along = term if along is None else along + term
        shape = base if along is None else base + along * (3.0 + 4.5 * along)
        entries.append(keep * h + scaled[WEIGHTS[d]] * shape)
    return entries


def collide(mom, pot, grad, states, tau, flip=None):
    inverse = 1.0 / mom[0]
    push = (-tau * COUPLING) * pot
    velocity = [(mom[1 + a] + push * grad[a]) * inverse for a in range(3)]
    if flip is not None:
        velocity[0] = velocity[0] * flip
    return relax(mom[0], velocity, states, 1.0 - 1.0 / tau, 1.0 / tau)


def fine_y(tiles, step, ghost):
    e = lane() & 15
    out = [None] * 8
    edge, inner, outer = (15, 0, 1) if step > 0 else (0, 1, 0)
    for r in range(4):
        across = rot(tiles[outer * 4 + r], 15 * step)
        out[inner * 4 + r] = jnp.where(e == edge, across, rot(tiles[inner * 4 + r], -step))
        out[outer * 4 + r] = jnp.where(e == edge, ghost[r], rot(tiles[outer * 4 + r], -step))
    return out


def fine_z(tiles, step):
    c = lane() >> 4
    moved = [rot(t, -16 * step) for t in tiles]
    edge = 7 if step > 0 else 0
    return [jnp.where(c == edge, moved[j ^ 1], moved[j]) for j in range(len(tiles))]


def fine_x(tiles, step, rows):
    s = sub()
    out = [None] * 8
    for k in range(2):
        for h in range(2):
            low, high = k * 4 + h, k * 4 + 2 + h
            if step > 0:
                out[low] = tiles[high]
                out[high] = jnp.where(s == 7, rows(4 + k * 2 + h), turn(tiles[low], -1))
            else:
                out[high] = tiles[low]
                out[low] = jnp.where(s == 0, rows(k * 2 + h), turn(tiles[high], 1))
    return out


def side_y(tile, step, ghost):
    e, k = lane() & 15, (sub() >> 1) & 1
    edge, inner = (15, 0) if step > 0 else (0, 1)
    across = turn(rot(tile, 15 * step), -2 * step)
    return jnp.where(e == edge, jnp.where(k == inner, across, ghost), rot(tile, -step))


def side_z(tile, step):
    c, h = lane() >> 4, sub() & 1
    moved = rot(tile, -16 * step)
    other = jnp.where(h == 0, turn(moved, -1), turn(moved, 1))
    return jnp.where(c == (7 if step > 0 else 0), other, moved)


def stencil(pot, up, down, back, front):
    total = pot * (1.0 / 18.0) + (up + down + back + front) * (1.0 / 36.0)
    return total, up - down, back - front


def rowcast(row):
    return jnp.broadcast_to(row, (8, 128))


def fine_step(state, mom, ghost_pot, ghost_post, ghost_side, halo, put, work):
    post, tee, face, rows = work
    pots = [mom[4, j] for j in range(8)]
    gp = [ghost_pot[h] for h in range(2)] * 2
    gz = fine_z(gp, 1)
    gz = [a - b for a, b in zip(gz, fine_z(gp, -1))]
    up, down = fine_y(pots, 1, gp), fine_y(pots, -1, gp)
    back, front = fine_z(pots, 1), fine_z(pots, -1)
    parts = [stencil(*v) for v in zip(pots, up, down, back, front)]
    total, dy, dz = ([p[i] for p in parts] for i in range(3))
    zz = [a + b for a, b in zip(fine_z(dy, 1), fine_z(dy, -1))]
    yy = [a + b for a, b in zip(fine_y(dz, 1, gz), fine_y(dz, -1, gz))]
    for j in range(8):
        tee[0, j] = total[j]
        tee[1, j] = dy[j] * (1.0 / 18.0) + zz[j] * (1.0 / 36.0)
        tee[2, j] = dz[j] * (1.0 / 18.0) + yy[j] * (1.0 / 36.0)
        tee[3, j] = dy[j]
        tee[4, j] = dz[j]

    def finish():
        flip = jnp.where(sub() < 4, 1.0, -1.0)
        near, far, own = potential(halo[0]), halo[9], face[...]
        outer, inner = ghost_side[0], ghost_side[1]

        def terms(tile, ghost):
            return stencil(tile, side_y(tile, 1, ghost), side_y(tile, -1, ghost), side_z(tile, 1), side_z(tile, -1))

        t1, y1, z1 = terms(near, outer)
        t2, y2, z2 = terms(far, outer)
        t0, y0, z0 = terms(own, inner)
        goz = side_z(outer, 1) - side_z(outer, -1)
        grad = [
            (t0 - t2) * flip,
            y1 * (1.0 / 18.0) + (y0 + y2 + side_z(y1, 1) + side_z(y1, -1)) * (1.0 / 36.0),
            z1 * (1.0 / 18.0) + (z0 + z2 + side_y(z1, 1, goz) + side_y(z1, -1, goz)) * (1.0 / 36.0),
        ]
        states = [(d, halo[4 + q]) for q, d in enumerate(X_PLUS)]
        for q, v in enumerate(collide([halo[i] for i in range(4)], near, grad, states, FINE_TAU, flip)):
            rows[q] = v
        rows[5], rows[6], rows[7] = t1, y1, z1

        def row(i):
            return lambda r: rowcast(rows[i, r : r + 1, :])

        total, dy, dz = ([tee[i, j] for j in range(8)] for i in (0, 3, 4))
        gx = [a - b for a, b in zip(fine_x(total, 1, row(5)), fine_x(total, -1, row(5)))]
        xy = [a + b for a, b in zip(fine_x(dy, 1, row(6)), fine_x(dy, -1, row(6)))]
        xz = [a + b for a, b in zip(fine_x(dz, 1, row(7)), fine_x(dz, -1, row(7)))]
        for j in range(8):
            tee[0, j] = gx[j]
            tee[1, j] = tee[1, j] + xy[j] * (1.0 / 36.0)
            tee[2, j] = tee[2, j] + xz[j] * (1.0 / 36.0)

        def body(j, _):
            values = collide(
                [mom[i, j] for i in range(4)],
                mom[4, j],
                [tee[i, j] for i in range(3)],
                [(d, state[d, j]) for d in range(19)],
                FINE_TAU,
            )
            for d in range(19):
                post[d, j] = values[d]
            return 0

        lax.fori_loop(0, 8, body, 0)
        for d in range(19):
            tiles = [post[d, j] for j in range(8)]
            cx, cy, cz = VELOCITIES[d]
            if cx:
                tiles = fine_x(tiles, -cx, row((X_PLUS if cx > 0 else X_MINUS).index(d)))
            if cz:
                tiles = fine_z(tiles, -cz)
            if cy:
                q = (Y_PLUS if cy > 0 else Y_MINUS).index(d)
                tiles = fine_y(tiles, -cy, [ghost_post[q, r] for r in range(4)])
            put(d, tiles)

    return finish


def fine_moments(state, mom):
    def body(j, _):
        values = moments([state[d, j] for d in range(19)])
        for i in range(4):
            mom[i, j] = values[i]
        mom[4, j] = potential(values[0])
        return 0

    lax.fori_loop(0, 8, body, 0)


def fine_faces(state, mom, out, face):
    for k in range(2):
        for h in range(2):
            r, low, high = k * 2 + h, k * 4 + h, k * 4 + 2 + h
            for i in range(4):
                out[i, r : r + 1, :] = mom[i, high, 7:8, :]
                out[i, 4 + r : 5 + r, :] = mom[i, low, 0:1, :]
            for q in range(5):
                out[4 + q, r : r + 1, :] = state[X_PLUS[q], high, 7:8, :]
                out[4 + q, 4 + r : 5 + r, :] = state[X_MINUS[q], low, 0:1, :]
            out[9, r : r + 1, :] = mom[4, low, 7:8, :]
            out[9, 4 + r : 5 + r, :] = mom[4, high, 0:1, :]
            face[r : r + 1, :] = mom[4, low, 0:1, :]
            face[4 + r : 5 + r, :] = mom[4, high, 7:8, :]


def kernel(
    fine, coarse, slots, fine_out, coarse_out,
    p1, r1, p2, r2, inv_v, inv_s,
    state, post, mom, tee, face, rows, out1, out2, halo1, halo2,
    layers, low_out, low_in, ghost, edge_r, edge_l, edge_in, ghost_post, ghost_side,
    cmom, face_c, halo_c, rest, rest_out, rest_in, ghost_t, ghost_c, ctee, cpost,
    s1, s2, s3, sg, se, sc, sm, sh1, sh2, sr, sx,
):
    g, w = lax.axis_index("grp"), lax.axis_index("wide")
    me = g * 32 + w
    right, left = lax.rem(g + 1, 4), lax.rem(g + 3, 4)
    ahead, behind = lax.rem(w + 1, 32), lax.rem(w + 31, 32)
    barrier = pltpu.get_barrier_semaphore()
    for offset in OFFSETS:
        pl.semaphore_signal(barrier, inc=1, device_id=device_of(offset), device_id_type=pl.DeviceIdType.MESH)

    def pack(t, _):
        for k in range(2):
            v = fine[k, :, pl.ds(pl.multiple_of(t * 128, 128), 128)]
            for q in range(4):
                n = min(5, 19 - 5 * q)
                p1[k, t * 4 + q, 0:n, :] = v[5 * q : 5 * q + n]
        return 0

    lax.fori_loop(0, 32, pack, 0)

    place = sub() * 128 + lane()

    def invert(b, acc):
        return jnp.where(place == slots[b], b, acc)

    inv_v[...] = lax.fori_loop(0, 256, invert, jnp.zeros((8, 128), jnp.int32), unroll=8)
    fetch = pltpu.make_async_copy(inv_v, inv_s, s3)
    fetch.start()
    for k in range(2):
        r1[2 * me + k, 0:5, :] = p1[k, me, 0:5, :]

    def coarse_body(i, _):
        values = moments([coarse[d, i] for d in range(19)])
        for a in range(4):
            cmom[a, i + 2] = values[a]
        cmom[4, i + 2] = potential(values[0])
        return 0

    lax.fori_loop(0, 8, coarse_body, 0)
    for q in range(5):
        face_c[0, q] = coarse[X_PLUS[q], 7]
        face_c[1, q] = coarse[X_MINUS[q], 0]

    flat = coarse.reshape(19 * 64, 128)
    e, c_l, s = lane() & 15, lane() >> 4, sub()

    def layer_body(d, _):
        for h in range(2):
            v = None
            for m in range(4):
                t = rot(flat[pl.ds(d * 64 + h * 4 + m, 8, stride=8), :], 32 * m + 15)
                v = t if v is None else jnp.where(c_l >= 2 * m, t, v)
            layers[d, h] = v
        return 0

    lax.fori_loop(0, 19, layer_body, 0)

    def rescaled(source, is_low, factor, h):
        m = moments([source[d, h] for d in range(19)])
        inverse = 1.0 / m[0]
        u = [m[1] * inverse, m[2] * inverse * jnp.where(is_low, 1.0, -1.0), m[3] * inverse]
        states = [(d, jnp.where(is_low, source[d, h], source[Y_MINUS[q], h])) for q, d in enumerate(Y_PLUS)]
        return relax(m[0], u, states, factor, 1.0 - factor) + [potential(m[0])]

    for h in range(2):
        for q, v in enumerate(rescaled(layers, e == 14, TO_FINE, h)):
            low_out[q, h] = jnp.where((c_l & 1) == 1, rot(v, 16), v)

    pl.semaphore_wait(barrier, len(OFFSETS))
    to_ahead = send(low_out, low_in, sg, (g, ahead))
    to_ahead.start()
    for offset in OFFSETS:
        x, y = device_of(offset)
        send(p1.at[:, x * 32 + y, 0:5, :], r1.at[pl.ds(2 * me, 2), 0:5, :], s1, (x, y)).start()
    cm_r = send(cmom.at[:, 8:10], cmom.at[:, 0:2], sm.at[0], (right, w))
    cm_l = send(cmom.at[:, 2:4], cmom.at[:, 10:12], sm.at[1], (left, w))
    cf_r = send(face_c.at[0], halo_c.at[0], sc.at[0], (right, w))
    cf_l = send(face_c.at[1], halo_c.at[1], sc.at[1], (left, w))
    for copy in (cm_r, cm_l, cf_r, cf_l):
        copy.start()

    to_ahead.wait()
    for q in range(6):
        for h in range(2):
            v = jnp.where(e == 0, rot(low_in[q, h], -14), low_out[q, h])
            ghost[q, h] = v
            edge_r[q * 2 + h : q * 2 + h + 1, :] = v[7:8]
            edge_l[q * 2 + h : q * 2 + h + 1, :] = v[0:1]
    ge_r = send(edge_r, edge_in.at[0], se.at[0], (right, w))
    ge_l = send(edge_l, edge_in.at[1], se.at[1], (left, w))
    ge_r.start()
    ge_l.start()

    fetch.wait()
    all1 = r1.at[0:254, 0:5, :]
    pltpu.make_async_copy(all1, all1, s1.at[1]).wait()

    def permute(m, _):
        for k in range(2):
            slot = 2 * m + k
            p2[k, m, 0:5, :] = r1[inv_s[slot // 128, lax.rem(slot, 128)], 0:5, :]
        return 0

    lax.fori_loop(0, 128, permute, 0, unroll=4)
    for k in range(2):
        r2[k, me, 0:5, :] = p2[k, me, 0:5, :]
    for offset in OFFSETS:
        x, y = device_of(offset)
        send(p2.at[:, x * 32 + y, 0:5, :], r2.at[:, me, 0:5, :], s2, (x, y)).start()

    ge_r.wait()
    ge_l.wait()
    for q in range(5):
        v = [ghost[q, h] for h in range(2)]
        cx, _, cz = VELOCITIES[Y_PLUS[q]]
        if cz:
            v = fine_z(v, -cz)
        for h in range(2):
            low = high = v[h]
            if cx > 0:
                low = jnp.where(s == 0, rowcast(edge_in[0, q * 2 + h : q * 2 + h + 1, :]), turn(v[h], 1))
            if cx < 0:
                high = jnp.where(s == 7, rowcast(edge_in[1, q * 2 + h : q * 2 + h + 1, :]), turn(v[h], -1))
            ghost_post[q, h] = low
            ghost_post[q, 2 + h] = high
    for k in range(2):
        for h in range(2):
            r = k * 2 + h
            ghost_side[0, r : r + 1, :] = edge_in[0, 10 + h : 11 + h, :]
            ghost_side[0, 4 + r : 5 + r, :] = edge_in[1, 10 + h : 11 + h, :]
            ghost_side[1, r : r + 1, :] = ghost[5, h, 0:1, :]
            ghost_side[1, 4 + r : 5 + r, :] = ghost[5, h, 7:8, :]
    for copy in (cm_r, cm_l, cf_r, cf_l):
        copy.wait()

    all2 = r2.at[:, 0:127, 0:5, :]
    pltpu.make_async_copy(all2, all2, s2.at[1]).wait()
    got = r2.reshape(2048, 128)
    for d in range(19):
        for k in range(2):
            for r in range(4):
                state[d, k * 4 + r] = got[pl.ds(((k * 128 + r * 4 + d // 5) * 8) + d % 5, 8, stride=128), :]

    fine_moments(state, mom)
    fine_faces(state, mom, out1, face)
    f1r = send(out1.at[:, 0:4], halo1.at[:, 0:4], sh1.at[0], (right, w))
    f1l = send(out1.at[:, 4:8], halo1.at[:, 4:8], sh1.at[1], (left, w))
    f1r.start()
    f1l.start()

    for d in range(19):
        for h in range(2):
            v = jnp.where(e < 8, state[d, h] + state[d, 2 + h], state[d, 4 + h] + state[d, 6 + h])
            v = v + rot(v, -1)
            rest[d, h] = 0.125 * (v + rot(v, -16))
    for h in range(2):
        for q, v in enumerate(rescaled(rest, e == 14, TO_COARSE, h)):
            rest_out[q, h] = v
    to_behind = send(rest_out, rest_in, sr, (g, behind))
    to_behind.start()

    work = (post, tee, face, rows)

    def keep(d, tiles):
        for j in range(8):
            state[d, j] = tiles[j]

    def give(d, tiles):
        for k in range(2):
            for r in range(4):
                fine_out[pl.ds(((k * 3 + d // 8) * 32 + r) * 8 + d % 8, 8, stride=32), :] = tiles[k * 4 + r]

    ghost_pot = [ghost[5, h] for h in range(2)]
    finish = fine_step(state, mom, ghost_pot, ghost_post, ghost_side, halo1, keep, work)
    f1r.wait()
    f1l.wait()
    finish()
    fine_moments(state, mom)
    fine_faces(state, mom, out2, face)
    f2r = send(out2.at[:, 0:4], halo2.at[:, 0:4], sh2.at[0], (right, w))
    f2l = send(out2.at[:, 4:8], halo2.at[:, 4:8], sh2.at[1], (left, w))
    f2r.start()
    f2l.start()

    to_behind.wait()
    turned = ghost_t.reshape(6 * 64, 128)
    last = lane() == 127
    for q in range(6):
        for h in range(2):
            for m in range(4):
                low = rot(rest_out[q, h], -(32 * m + 14))
                ghost_t[q, h * 4 + m] = jnp.where(last, rot(rest_in[q, h], 127 - 32 * m), low)
        for x in range(8):
            ghost_c[q, x + 2] = turned[pl.ds(q * 64 + x, 8, stride=8), :]
    gc_r = send(ghost_c.at[:, 8:10], ghost_c.at[:, 0:2], sx.at[0], (right, w))
    gc_l = send(ghost_c.at[:, 2:4], ghost_c.at[:, 10:12], sx.at[1], (left, w))
    gc_r.start()
    gc_l.start()

    finish = fine_step(state, mom, ghost_pot, ghost_post, ghost_side, halo2, give, work)
    f2r.wait()
    f2l.wait()
    finish()

    gc_r.wait()
    gc_l.wait()

    def coarse_y(v, step, edge):
        return jnp.where(lane() == (127 if step > 0 else 0), edge, rot(v, -step))

    def terms_body(i, _):
        v, edge = cmom[4, i], ghost_c[5, i]
        t, dy, dz = stencil(v, coarse_y(v, 1, edge), coarse_y(v, -1, edge), turn(v, -1), turn(v, 1))
        ctee[0, i], ctee[1, i], ctee[2, i] = t, dy, dz
        return 0

    lax.fori_loop(0, 12, terms_body, 0)

    def coarse_grad(i):
        dy, dz, edge = ctee[1, i], ctee[2, i], ghost_c[5, i]
        edge = turn(edge, -1) - turn(edge, 1)
        return [
            ctee[0, i + 1] - ctee[0, i - 1],
            dy * (1.0 / 18.0) + (ctee[1, i + 1] + ctee[1, i - 1] + turn(dy, 1) + turn(dy, -1)) * (1.0 / 36.0),
            dz * (1.0 / 18.0)
            + (ctee[2, i + 1] + ctee[2, i - 1] + coarse_y(dz, 1, edge) + coarse_y(dz, -1, edge)) * (1.0 / 36.0),
        ]

    def coarse_post(i, states):
        values = collide([cmom[a, i] for a in range(4)], cmom[4, i], coarse_grad(i), states, COARSE_TAU)
        for (d, _), v in zip(states, values):
            cpost[d, i - 1] = v

    def post_body(i, _):
        coarse_post(i + 2, [(d, coarse[d, i]) for d in range(19)])
        return 0

    lax.fori_loop(0, 8, post_body, 0)
    coarse_post(1, [(d, halo_c[0, q]) for q, d in enumerate(X_PLUS)])
    coarse_post(10, [(d, halo_c[1, q]) for q, d in enumerate(X_MINUS)])

    def stream_body(i, _):
        for d in range(19):
            cx, cy, cz = VELOCITIES[d]
            v = cpost[d, i + 1 - cx]
            if cz:
                v = turn(v, cz)
            if cy:
                edge = ghost_c[(Y_PLUS if cy > 0 else Y_MINUS).index(d), i + 2 - cx]
                v = coarse_y(v, -cy, turn(edge, cz) if cz else edge)
            coarse_out[d, i] = v
        return 0

    lax.fori_loop(0, 8, stream_body, 0)
    pltpu.make_async_copy(all1, all1, s1.at[0]).wait()
    pltpu.make_async_copy(all2, all2, s2.at[0]).wait()


def local(fine_pop, coarse_pop, new_slot):
    def tiles(*shape):
        return pltpu.VMEM(shape + (8, 128), jnp.float32)

    def sems(*shape):
        return pltpu.SemaphoreType.DMA(shape)

    vmem = pl.BlockSpec(memory_space=pltpu.VMEM)
    fine_out, coarse_out = pl.pallas_call(
        kernel,
        out_shape=(
            jax.ShapeDtypeStruct((1536, 128), jnp.float32),
            jax.ShapeDtypeStruct((19, 8, 8, 128), jnp.float32),
        ),
        in_specs=[vmem, vmem, pl.BlockSpec(memory_space=pltpu.SMEM)],
        out_specs=(vmem, vmem),
        scratch_shapes=[
            tiles(2, 128), tiles(256), tiles(2, 128), tiles(2, 128),
            pltpu.VMEM((8, 128), jnp.int32), pltpu.SMEM((8, 128), jnp.int32),
            tiles(19, 8), tiles(19, 8), tiles(5, 8), tiles(5, 8), tiles(), tiles(8),
            tiles(10), tiles(10), tiles(10), tiles(10),
            tiles(19, 2), tiles(6, 2), tiles(6, 2), tiles(6, 2),
            pltpu.VMEM((12, 128), jnp.float32), pltpu.VMEM((12, 128), jnp.float32),
            pltpu.VMEM((2, 12, 128), jnp.float32), tiles(5, 4), tiles(2),
            tiles(5, 12), tiles(2, 5), tiles(2, 5), tiles(19, 2), tiles(6, 2), tiles(6, 2),
            tiles(6, 8), tiles(6, 12), tiles(3, 12), tiles(19, 10),
            sems(2), sems(2), pltpu.SemaphoreType.DMA, sems(2), sems(2, 2), sems(2, 2), sems(2, 2),
            sems(2, 2), sems(2, 2), sems(2), sems(2, 2),
        ],
        compiler_params=pltpu.CompilerParams(
            collective_id=0, has_side_effects=True, vmem_limit_bytes=48 * 2**20
        ),
    )(fine_pop, coarse_pop, new_slot)
    fine_out = fine_out.reshape(2, 3, 32, 8, 128).transpose(0, 1, 3, 2, 4).reshape(2, 24, 4096)[:, :19]
    return fine_out, coarse_out


def solution(mesh):
    return jax.shard_map(
        local,
        mesh=mesh,
        in_specs=(P(("grp", "wide"), None, None), P(None, "grp", None, "wide"), P()),
        out_specs=(P(("grp", "wide"), None, None), P(None, "grp", None, "wide")),
        check_vma=False,
    )
```

```python
import jax
import jax.numpy as jnp
from jax import lax
from jax.experimental import pallas as pl
from jax.experimental.pallas import tpu as pltpu
from jax.sharding import PartitionSpec as P

VELOCITIES = (
    (0, 0, 0),
    (1, 0, 0),
    (-1, 0, 0),
    (0, 1, 0),
    (0, -1, 0),
    (0, 0, 1),
    (0, 0, -1),
    (1, 1, 0),
    (-1, -1, 0),
    (1, -1, 0),
    (-1, 1, 0),
    (1, 0, 1),
    (-1, 0, -1),
    (1, 0, -1),
    (-1, 0, 1),
    (0, 1, 1),
    (0, -1, -1),
    (0, 1, -1),
    (0, -1, 1),
)
WEIGHTS = (1.0 / 3.0,) + (1.0 / 18.0,) * 6 + (1.0 / 36.0,) * 12
COUPLING = -5.0
FINE_TAU = 1.1
COARSE_TAU = 0.8
TO_COARSE = 2.0 * COARSE_TAU / FINE_TAU
TO_FINE = FINE_TAU / (2.0 * COARSE_TAU)

INDEX = {c: i for i, c in enumerate(VELOCITIES)}
X_PLUS = (1, 7, 9, 11, 13)
X_MINUS = tuple(INDEX[(-c[0], c[1], c[2])] for c in (VELOCITIES[i] for i in X_PLUS))
Y_PLUS = (3, 7, 10, 15, 17)
Y_MINUS = tuple(INDEX[(c[0], -c[1], c[2])] for c in (VELOCITIES[i] for i in Y_PLUS))

OFFSETS = sorted(
    ((a, b, c, d) for a in range(4) for b in range(4) for c in range(4) for d in range(2) if a + b + c + d),
    key=lambda o: (-sum(min(v, 4 - v) for v in o[:3]), (o[0] * 7 + o[1] * 5 + o[2] * 3 + o[3]) % 11),
)


def send(src, dst, sems, device):
    return pltpu.make_async_remote_copy(
        src_ref=src,
        dst_ref=dst,
        send_sem=sems.at[0],
        recv_sem=sems.at[1],
        device_id=device,
        device_id_type=pl.DeviceIdType.MESH,
    )


def device_of(offset):
    g, w = lax.axis_index("grp"), lax.axis_index("wide")
    x = lax.rem(g + offset[0], 4)
    y = lax.rem(w // 8 + offset[1], 4)
    z = lax.rem(lax.rem(w // 2, 4) + offset[2], 4)
    c = lax.rem(lax.rem(w, 2) + offset[3], 2)
    return x, (y * 4 + z) * 2 + c


def lane():
    return lax.broadcasted_iota(jnp.int32, (8, 128), 1)


def sub():
    return lax.broadcasted_iota(jnp.int32, (8, 128), 0)


def rot(v, shift):
    return pltpu.roll(v, shift % 128, 1)


def turn(v, shift):
    return pltpu.roll(v, shift % 8, 0)


def potential(density):
    return 1.0 - jnp.exp(-density)


def moments(state):
    density = state[0]
    momentum = [None, None, None]
    for d in range(1, 19):
        density = density + state[d]
        for a in range(3):
            c = VELOCITIES[d][a]
            if c:
                m = momentum[a]
                momentum[a] = c * state[d] if m is None else (m + state[d] if c > 0 else m - state[d])
    return [density] + momentum


def relax(density, velocity, states, keep, gain):
    base = 1.0 - 1.5 * (velocity[0] * velocity[0] + velocity[1] * velocity[1] + velocity[2] * velocity[2])
    scaled = {w: (gain * w) * density for w in set(WEIGHTS[d] for d, _ in states)}
    entries = []
    for d, h in states:
        along = None
        for a in range(3):
            c = VELOCITIES[d][a]
            if c:
                term = velocity[a] if c > 0 else -velocity[a]
                along = term if along is None else along + term
        shape = base if along is None else base + along * (3.0 + 4.5 * along)
        entries.append(keep * h + scaled[WEIGHTS[d]] * shape)
    return entries


def collide(mom, pot, grad, states, tau, flip=None):
    inverse = 1.0 / mom[0]
    push = (-tau * COUPLING) * pot
    velocity = [(mom[1 + a] + push * grad[a]) * inverse for a in range(3)]
    if flip is not None:
        velocity[0] = velocity[0] * flip
    return relax(mom[0], velocity, states, 1.0 - 1.0 / tau, 1.0 / tau)


def fine_y(tiles, step, ghost):
    e = lane() & 15
    out = [None] * 8
    edge, inner, outer = (15, 0, 1) if step > 0 else (0, 1, 0)
    for r in range(4):
        across = rot(tiles[outer * 4 + r], 15 * step)
        out[inner * 4 + r] = jnp.where(e == edge, across, rot(tiles[inner * 4 + r], -step))
        out[outer * 4 + r] = jnp.where(e == edge, ghost[r], rot(tiles[outer * 4 + r], -step))
    return out


def fine_z(tiles, step):
    c = lane() >> 4
    moved = [rot(t, -16 * step) for t in tiles]
    edge = 7 if step > 0 else 0
    return [jnp.where(c == edge, moved[j ^ 1], moved[j]) for j in range(len(tiles))]


def fine_x(tiles, step, rows):
    s = sub()
    out = [None] * 8
    for k in range(2):
        for h in range(2):
            low, high = k * 4 + h, k * 4 + 2 + h
            if step > 0:
                out[low] = tiles[high]
                out[high] = jnp.where(s == 7, rows(4 + k * 2 + h), turn(tiles[low], -1))
            else:
                out[high] = tiles[low]
                out[low] = jnp.where(s == 0, rows(k * 2 + h), turn(tiles[high], 1))
    return out


def side_y(tile, step, ghost):
    e, k = lane() & 15, (sub() >> 1) & 1
    edge, inner = (15, 0) if step > 0 else (0, 1)
    across = turn(rot(tile, 15 * step), -2 * step)
    return jnp.where(e == edge, jnp.where(k == inner, across, ghost), rot(tile, -step))


def side_z(tile, step):
    c, h = lane() >> 4, sub() & 1
    moved = rot(tile, -16 * step)
    other = jnp.where(h == 0, turn(moved, -1), turn(moved, 1))
    return jnp.where(c == (7 if step > 0 else 0), other, moved)


def stencil(pot, up, down, back, front):
    total = pot * (1.0 / 18.0) + (up + down + back + front) * (1.0 / 36.0)
    return total, up - down, back - front


def rowcast(row):
    return jnp.broadcast_to(row, (8, 128))


def fine_step(state, mom, ghost_pot, ghost_post, ghost_side, halo, put, work):
    post, tee, face, rows = work
    pots = [mom[4, j] for j in range(8)]
    gp = [ghost_pot[h] for h in range(2)] * 2
    gz = fine_z(gp, 1)
    gz = [a - b for a, b in zip(gz, fine_z(gp, -1))]
    up, down = fine_y(pots, 1, gp), fine_y(pots, -1, gp)
    back, front = fine_z(pots, 1), fine_z(pots, -1)
    parts = [stencil(*v) for v in zip(pots, up, down, back, front)]
    total, dy, dz = ([p[i] for p in parts] for i in range(3))
    zz = [a + b for a, b in zip(fine_z(dy, 1), fine_z(dy, -1))]
    yy = [a + b for a, b in zip(fine_y(dz, 1, gz), fine_y(dz, -1, gz))]
    for j in range(8):
        tee[0, j] = total[j]
        tee[1, j] = dy[j] * (1.0 / 18.0) + zz[j] * (1.0 / 36.0)
        tee[2, j] = dz[j] * (1.0 / 18.0) + yy[j] * (1.0 / 36.0)
        tee[3, j] = dy[j]
        tee[4, j] = dz[j]

    def finish():
        flip = jnp.where(sub() < 4, 1.0, -1.0)
        near, far, own = potential(halo[0]), halo[9], face[...]
        outer, inner = ghost_side[0], ghost_side[1]

        def terms(tile, ghost):
            return stencil(tile, side_y(tile, 1, ghost), side_y(tile, -1, ghost), side_z(tile, 1), side_z(tile, -1))

        t1, y1, z1 = terms(near, outer)
        t2, y2, z2 = terms(far, outer)
        t0, y0, z0 = terms(own, inner)
        goz = side_z(outer, 1) - side_z(outer, -1)
        grad = [
            (t0 - t2) * flip,
            y1 * (1.0 / 18.0) + (y0 + y2 + side_z(y1, 1) + side_z(y1, -1)) * (1.0 / 36.0),
            z1 * (1.0 / 18.0) + (z0 + z2 + side_y(z1, 1, goz) + side_y(z1, -1, goz)) * (1.0 / 36.0),
        ]
        states = [(d, halo[4 + q]) for q, d in enumerate(X_PLUS)]
        for q, v in enumerate(collide([halo[i] for i in range(4)], near, grad, states, FINE_TAU, flip)):
            rows[q] = v
        rows[5], rows[6], rows[7] = t1, y1, z1

        def row(i):
            return lambda r: rowcast(rows[i, r : r + 1, :])

        total, dy, dz = ([tee[i, j] for j in range(8)] for i in (0, 3, 4))
        gx = [a - b for a, b in zip(fine_x(total, 1, row(5)), fine_x(total, -1, row(5)))]
        xy = [a + b for a, b in zip(fine_x(dy, 1, row(6)), fine_x(dy, -1, row(6)))]
        xz = [a + b for a, b in zip(fine_x(dz, 1, row(7)), fine_x(dz, -1, row(7)))]
        for j in range(8):
            tee[0, j] = gx[j]
            tee[1, j] = tee[1, j] + xy[j] * (1.0 / 36.0)
            tee[2, j] = tee[2, j] + xz[j] * (1.0 / 36.0)

        def body(j, _):
            values = collide(
                [mom[i, j] for i in range(4)],
                mom[4, j],
                [tee[i, j] for i in range(3)],
                [(d, state[d, j]) for d in range(19)],
                FINE_TAU,
            )
            for d in range(19):
                post[d, j] = values[d]
            return 0

        lax.fori_loop(0, 8, body, 0)
        for d in range(19):
            tiles = [post[d, j] for j in range(8)]
            cx, cy, cz = VELOCITIES[d]
            if cx:
                tiles = fine_x(tiles, -cx, row((X_PLUS if cx > 0 else X_MINUS).index(d)))
            if cz:
                tiles = fine_z(tiles, -cz)
            if cy:
                q = (Y_PLUS if cy > 0 else Y_MINUS).index(d)
                tiles = fine_y(tiles, -cy, [ghost_post[q, r] for r in range(4)])
            put(d, tiles)

    return finish


def fine_moments(state, mom):
    def body(j, _):
        values = moments([state[d, j] for d in range(19)])
        for i in range(4):
            mom[i, j] = values[i]
        mom[4, j] = potential(values[0])
        return 0

    lax.fori_loop(0, 8, body, 0)


def fine_faces(state, mom, out, face):
    for k in range(2):
        for h in range(2):
            r, low, high = k * 2 + h, k * 4 + h, k * 4 + 2 + h
            for i in range(4):
                out[i, r : r + 1, :] = mom[i, high, 7:8, :]
                out[i, 4 + r : 5 + r, :] = mom[i, low, 0:1, :]
            for q in range(5):
                out[4 + q, r : r + 1, :] = state[X_PLUS[q], high, 7:8, :]
                out[4 + q, 4 + r : 5 + r, :] = state[X_MINUS[q], low, 0:1, :]
            out[9, r : r + 1, :] = mom[4, low, 7:8, :]
            out[9, 4 + r : 5 + r, :] = mom[4, high, 0:1, :]
            face[r : r + 1, :] = mom[4, low, 0:1, :]
            face[4 + r : 5 + r, :] = mom[4, high, 7:8, :]


def kernel(
    fine_hbm, coarse_hbm, slots_hbm, fine_out, coarse_out,
    fine, coarse, slots, si, p1, r1, p2, r2, inv_v, inv_s,
    state, post, mom, tee, face, rows, out1, out2, halo1, halo2,
    layers, low_out, low_in, ghost, edge_r, edge_l, edge_in, ghost_post, ghost_side,
    cmom, face_c, halo_c, rest, rest_out, rest_in, ghost_t, ghost_c, ctee, cpost,
    s1, s2, s3, sg, se, sc, sm, sh1, sh2, sr, sx,
):
    g, w = lax.axis_index("grp"), lax.axis_index("wide")
    me = g * 32 + w
    right, left = lax.rem(g + 1, 4), lax.rem(g + 3, 4)
    ahead, behind = lax.rem(w + 1, 32), lax.rem(w + 31, 32)
    barrier = pltpu.get_barrier_semaphore()
    for offset in OFFSETS:
        pl.semaphore_signal(barrier, inc=1, device_id=device_of(offset), device_id_type=pl.DeviceIdType.MESH)

    loads = [pltpu.make_async_copy(*pair, si.at[i]) for i, pair in enumerate(((fine_hbm, fine), (slots_hbm, slots), (coarse_hbm, coarse)))]
    for load in loads:
        load.start()
    for load in loads:
        load.wait()

    def pack(t, _):
        for k in range(2):
            for q in range(4):
                n = min(5, 19 - 5 * q)
                p1[k, t * 4 + q, 0:n, :] = fine[pl.ds(5 * q * 64 + t * 2 + k, n, stride=64), :]
        return 0

    lax.fori_loop(0, 32, pack, 0)

    place = sub() * 128 + lane()

    def invert(b, acc):
        return jnp.where(place == slots[b], b, acc)

    inv_v[...] = lax.fori_loop(0, 256, invert, jnp.zeros((8, 128), jnp.int32), unroll=8)
    fetch = pltpu.make_async_copy(inv_v, inv_s, s3)
    fetch.start()
    for k in range(2):
        r1[2 * me + k, 0:5, :] = p1[k, me, 0:5, :]

    def coarse_body(i, _):
        values = moments([coarse[d, i] for d in range(19)])
        for a in range(4):
            cmom[a, i + 2] = values[a]
        cmom[4, i + 2] = potential(values[0])
        return 0

    lax.fori_loop(0, 8, coarse_body, 0)
    for q in range(5):
        face_c[0, q] = coarse[X_PLUS[q], 7]
        face_c[1, q] = coarse[X_MINUS[q], 0]

    flat = coarse.reshape(19 * 64, 128)
    e, c_l, s = lane() & 15, lane() >> 4, sub()

    def layer_body(d, _):
        for h in range(2):
            v = None
            for m in range(4):
                t = rot(flat[pl.ds(d * 64 + h * 4 + m, 8, stride=8), :], 32 * m + 15)
                v = t if v is None else jnp.where(c_l >= 2 * m, t, v)
            layers[d, h] = v
        return 0

    lax.fori_loop(0, 19, layer_body, 0)

    def rescaled(source, is_low, factor, h):
        m = moments([source[d, h] for d in range(19)])
        inverse = 1.0 / m[0]
        u = [m[1] * inverse, m[2] * inverse * jnp.where(is_low, 1.0, -1.0), m[3] * inverse]
        states = [(d, jnp.where(is_low, source[d, h], source[Y_MINUS[q], h])) for q, d in enumerate(Y_PLUS)]
        return relax(m[0], u, states, factor, 1.0 - factor) + [potential(m[0])]

    for h in range(2):
        for q, v in enumerate(rescaled(layers, e == 14, TO_FINE, h)):
            low_out[q, h] = jnp.where((c_l & 1) == 1, rot(v, 16), v)

    pl.semaphore_wait(barrier, len(OFFSETS))
    to_ahead = send(low_out, low_in, sg, (g, ahead))
    to_ahead.start()
    for offset in OFFSETS:
        x, y = device_of(offset)
        send(p1.at[:, x * 32 + y, 0:5, :], r1.at[pl.ds(2 * me, 2), 0:5, :], s1, (x, y)).start()
    cm_r = send(cmom.at[:, 8:10], cmom.at[:, 0:2], sm.at[0], (right, w))
    cm_l = send(cmom.at[:, 2:4], cmom.at[:, 10:12], sm.at[1], (left, w))
    cf_r = send(face_c.at[0], halo_c.at[0], sc.at[0], (right, w))
    cf_l = send(face_c.at[1], halo_c.at[1], sc.at[1], (left, w))
    for copy in (cm_r, cm_l, cf_r, cf_l):
        copy.start()

    to_ahead.wait_recv()
    for q in range(6):
        for h in range(2):
            v = jnp.where(e == 0, rot(low_in[q, h], -14), low_out[q, h])
            ghost[q, h] = v
            edge_r[q * 2 + h : q * 2 + h + 1, :] = v[7:8]
            edge_l[q * 2 + h : q * 2 + h + 1, :] = v[0:1]
    ge_r = send(edge_r, edge_in.at[0], se.at[0], (right, w))
    ge_l = send(edge_l, edge_in.at[1], se.at[1], (left, w))
    ge_r.start()
    ge_l.start()

    fetch.wait()
    all1 = r1.at[0:254, 0:5, :]
    pltpu.make_async_copy(all1, all1, s1.at[1]).wait()

    for start in range(0, 128, 8):
        group = ([(0, 0, 0, 0)] + OFFSETS)[start : start + 8]
        targets = [device_of(offset) for offset in group]
        owners = [x * 32 + y for x, y in targets]
        found = [[inv_s[m // 64, 2 * lax.rem(m, 64) + k] for k in range(2)] for m in owners]
        pieces = [[r1[b, 0:5, :] for b in pair] for pair in found]
        for m, pair in zip(owners, pieces):
            for k in range(2):
                p2[k, m, 0:5, :] = pair[k]
        for m, pair, offset, device in zip(owners, pieces, group, targets):
            if any(offset):
                send(p2.at[:, m, 0:5, :], r2.at[:, me, 0:5, :], s2, device).start()
            else:
                for k in range(2):
                    r2[k, me, 0:5, :] = pair[k]

    ge_r.wait_recv()
    ge_l.wait_recv()
    for q in range(5):
        v = [ghost[q, h] for h in range(2)]
        cx, _, cz = VELOCITIES[Y_PLUS[q]]
        if cz:
            v = fine_z(v, -cz)
        for h in range(2):
            low = high = v[h]
            if cx > 0:
                low = jnp.where(s == 0, rowcast(edge_in[0, q * 2 + h : q * 2 + h + 1, :]), turn(v[h], 1))
            if cx < 0:
                high = jnp.where(s == 7, rowcast(edge_in[1, q * 2 + h : q * 2 + h + 1, :]), turn(v[h], -1))
            ghost_post[q, h] = low
            ghost_post[q, 2 + h] = high
    for k in range(2):
        for h in range(2):
            r = k * 2 + h
            ghost_side[0, r : r + 1, :] = edge_in[0, 10 + h : 11 + h, :]
            ghost_side[0, 4 + r : 5 + r, :] = edge_in[1, 10 + h : 11 + h, :]
            ghost_side[1, r : r + 1, :] = ghost[5, h, 0:1, :]
            ghost_side[1, 4 + r : 5 + r, :] = ghost[5, h, 7:8, :]
    for copy in (cm_r, cm_l, cf_r, cf_l):
        copy.wait_recv()

    all2 = r2.at[:, 0:127, 0:5, :]
    pltpu.make_async_copy(all2, all2, s2.at[1]).wait()
    got = r2.reshape(2048, 128)
    for d in range(19):
        for k in range(2):
            for r in range(4):
                state[d, k * 4 + r] = got[pl.ds(((k * 128 + r * 4 + d // 5) * 8) + d % 5, 8, stride=128), :]

    fine_moments(state, mom)
    fine_faces(state, mom, out1, face)
    f1r = send(out1.at[:, 0:4], halo1.at[:, 0:4], sh1.at[0], (right, w))
    f1l = send(out1.at[:, 4:8], halo1.at[:, 4:8], sh1.at[1], (left, w))
    f1r.start()
    f1l.start()

    for d in range(19):
        for h in range(2):
            v = jnp.where(e < 8, state[d, h] + state[d, 2 + h], state[d, 4 + h] + state[d, 6 + h])
            v = v + rot(v, -1)
            rest[d, h] = 0.125 * (v + rot(v, -16))
    for h in range(2):
        for q, v in enumerate(rescaled(rest, e == 14, TO_COARSE, h)):
            rest_out[q, h] = v
    to_behind = send(rest_out, rest_in, sr, (g, behind))
    to_behind.start()

    work = (post, tee, face, rows)

    def keep(d, tiles):
        for j in range(8):
            state[d, j] = tiles[j]

    def give(d, tiles):
        for k in range(2):
            for r in range(4):
                fine_out[pl.ds(d * 64 + r * 2 + k, 8, stride=8), :] = tiles[k * 4 + r]

    ghost_pot = [ghost[5, h] for h in range(2)]
    finish = fine_step(state, mom, ghost_pot, ghost_post, ghost_side, halo1, keep, work)
    f1r.wait_recv()
    f1l.wait_recv()
    finish()
    fine_moments(state, mom)
    fine_faces(state, mom, out2, face)
    f2r = send(out2.at[:, 0:4], halo2.at[:, 0:4], sh2.at[0], (right, w))
    f2l = send(out2.at[:, 4:8], halo2.at[:, 4:8], sh2.at[1], (left, w))
    f2r.start()
    f2l.start()

    to_behind.wait_recv()
    turned = ghost_t.reshape(6 * 64, 128)
    last = lane() == 127
    for q in range(6):
        for h in range(2):
            for m in range(4):
                low = rot(rest_out[q, h], -(32 * m + 14))
                ghost_t[q, h * 4 + m] = jnp.where(last, rot(rest_in[q, h], 127 - 32 * m), low)
        for x in range(8):
            ghost_c[q, x + 2] = turned[pl.ds(q * 64 + x, 8, stride=8), :]
    gc_r = send(ghost_c.at[:, 8:10], ghost_c.at[:, 0:2], sx.at[0], (right, w))
    gc_l = send(ghost_c.at[:, 2:4], ghost_c.at[:, 10:12], sx.at[1], (left, w))
    gc_r.start()
    gc_l.start()

    finish = fine_step(state, mom, ghost_pot, ghost_post, ghost_side, halo2, give, work)
    f2r.wait_recv()
    f2l.wait_recv()
    finish()

    gc_r.wait_recv()
    gc_l.wait_recv()

    def coarse_y(v, step, edge):
        return jnp.where(lane() == (127 if step > 0 else 0), edge, rot(v, -step))

    def terms_body(i, _):
        v, edge = cmom[4, i], ghost_c[5, i]
        t, dy, dz = stencil(v, coarse_y(v, 1, edge), coarse_y(v, -1, edge), turn(v, -1), turn(v, 1))
        ctee[0, i], ctee[1, i], ctee[2, i] = t, dy, dz
        return 0

    lax.fori_loop(0, 12, terms_body, 0)

    def coarse_grad(i):
        dy, dz, edge = ctee[1, i], ctee[2, i], ghost_c[5, i]
        edge = turn(edge, -1) - turn(edge, 1)
        return [
            ctee[0, i + 1] - ctee[0, i - 1],
            dy * (1.0 / 18.0) + (ctee[1, i + 1] + ctee[1, i - 1] + turn(dy, 1) + turn(dy, -1)) * (1.0 / 36.0),
            dz * (1.0 / 18.0)
            + (ctee[2, i + 1] + ctee[2, i - 1] + coarse_y(dz, 1, edge) + coarse_y(dz, -1, edge)) * (1.0 / 36.0),
        ]

    def coarse_post(i, states):
        values = collide([cmom[a, i] for a in range(4)], cmom[4, i], coarse_grad(i), states, COARSE_TAU)
        for (d, _), v in zip(states, values):
            cpost[d, i - 1] = v

    def post_body(i, _):
        coarse_post(i + 2, [(d, coarse[d, i]) for d in range(19)])
        return 0

    lax.fori_loop(0, 8, post_body, 0)
    coarse_post(1, [(d, halo_c[0, q]) for q, d in enumerate(X_PLUS)])
    coarse_post(10, [(d, halo_c[1, q]) for q, d in enumerate(X_MINUS)])

    def stream_body(i, _):
        for d in range(19):
            cx, cy, cz = VELOCITIES[d]
            v = cpost[d, i + 1 - cx]
            if cz:
                v = turn(v, cz)
            if cy:
                edge = ghost_c[(Y_PLUS if cy > 0 else Y_MINUS).index(d), i + 2 - cx]
                v = coarse_y(v, -cy, turn(edge, cz) if cz else edge)
            coarse_out[d, i] = v
        return 0

    lax.fori_loop(0, 8, stream_body, 0)
    for copy in (to_ahead, ge_r, ge_l, cm_r, cm_l, cf_r, cf_l, f1r, f1l, f2r, f2l, gc_r, gc_l, to_behind):
        copy.wait_send()
    pltpu.make_async_copy(all1, all1, s1.at[0]).wait()
    pltpu.make_async_copy(all2, all2, s2.at[0]).wait()


def local(fine_pop, coarse_pop, new_slot):
    def tiles(*shape):
        return pltpu.VMEM(shape + (8, 128), jnp.float32)

    def sems(*shape):
        return pltpu.SemaphoreType.DMA(shape)

    vmem = pl.BlockSpec(memory_space=pltpu.VMEM)
    fine_out, coarse_out = pl.pallas_call(
        kernel,
        out_shape=(
            jax.ShapeDtypeStruct((1216, 128), jnp.float32),
            jax.ShapeDtypeStruct((19, 8, 8, 128), jnp.float32),
        ),
        in_specs=[pl.BlockSpec(memory_space=pltpu.HBM)] * 3,
        out_specs=(vmem, vmem),
        scratch_shapes=[
            pltpu.VMEM((1216, 128), jnp.float32), tiles(19, 8), pltpu.SMEM((256,), jnp.int32), sems(3),
            tiles(2, 128), tiles(256), tiles(2, 128), tiles(2, 128),
            pltpu.VMEM((8, 128), jnp.int32), pltpu.SMEM((8, 128), jnp.int32),
            tiles(19, 8), tiles(19, 8), tiles(5, 8), tiles(5, 8), tiles(), tiles(8),
            tiles(10), tiles(10), tiles(10), tiles(10),
            tiles(19, 2), tiles(6, 2), tiles(6, 2), tiles(6, 2),
            pltpu.VMEM((12, 128), jnp.float32), pltpu.VMEM((12, 128), jnp.float32),
            pltpu.VMEM((2, 12, 128), jnp.float32), tiles(5, 4), tiles(2),
            tiles(5, 12), tiles(2, 5), tiles(2, 5), tiles(19, 2), tiles(6, 2), tiles(6, 2),
            tiles(6, 8), tiles(6, 12), tiles(3, 12), tiles(19, 10),
            sems(2), sems(2), pltpu.SemaphoreType.DMA, sems(2), sems(2, 2), sems(2, 2), sems(2, 2),
            sems(2, 2), sems(2, 2), sems(2), sems(2, 2),
        ],
        compiler_params=pltpu.CompilerParams(
            collective_id=0, has_side_effects=True, vmem_limit_bytes=53836 * 1024
        ),
    )(fine_pop.reshape(2, 19, 32, 128).transpose(1, 2, 0, 3).reshape(1216, 128), coarse_pop, new_slot)
    fine_out = fine_out.reshape(19, 32, 2, 128).transpose(2, 0, 1, 3).reshape(2, 19, 4096)
    return fine_out, coarse_out


def solution(mesh):
    return jax.shard_map(
        local,
        mesh=mesh,
        in_specs=(P(("grp", "wide"), None, None), P(None, "grp", None, "wide"), P()),
        out_specs=(P(("grp", "wide"), None, None), P(None, "grp", None, "wide")),
        check_vma=False,
    )
```

```python
import jax
import jax.numpy as jnp
from jax import lax
from jax.experimental import pallas as pl
from jax.experimental.pallas import tpu as pltpu
from jax.sharding import PartitionSpec as P

VELOCITIES = (
    (0, 0, 0),
    (1, 0, 0),
    (-1, 0, 0),
    (0, 1, 0),
    (0, -1, 0),
    (0, 0, 1),
    (0, 0, -1),
    (1, 1, 0),
    (-1, -1, 0),
    (1, -1, 0),
    (-1, 1, 0),
    (1, 0, 1),
    (-1, 0, -1),
    (1, 0, -1),
    (-1, 0, 1),
    (0, 1, 1),
    (0, -1, -1),
    (0, 1, -1),
    (0, -1, 1),
)
WEIGHTS = (1.0 / 3.0,) + (1.0 / 18.0,) * 6 + (1.0 / 36.0,) * 12
COUPLING = -5.0
FINE_TAU = 1.1
COARSE_TAU = 0.8
TO_COARSE = 2.0 * COARSE_TAU / FINE_TAU
TO_FINE = FINE_TAU / (2.0 * COARSE_TAU)

INDEX = {c: i for i, c in enumerate(VELOCITIES)}
X_PLUS = (1, 7, 9, 11, 13)
X_MINUS = tuple(INDEX[(-c[0], c[1], c[2])] for c in (VELOCITIES[i] for i in X_PLUS))
Y_PLUS = (3, 7, 10, 15, 17)
Y_MINUS = tuple(INDEX[(c[0], -c[1], c[2])] for c in (VELOCITIES[i] for i in Y_PLUS))

OFFSETS = sorted(
    ((a, b, c, d) for a in range(4) for b in range(4) for c in range(4) for d in range(2) if a + b + c + d),
    key=lambda o: (-sum(min(v, 4 - v) for v in o[:3]), (o[0] * 7 + o[1] * 5 + o[2] * 3 + o[3]) % 11),
)


def send(src, dst, sems, device):
    return pltpu.make_async_remote_copy(
        src_ref=src,
        dst_ref=dst,
        send_sem=sems.at[0],
        recv_sem=sems.at[1],
        device_id=device,
        device_id_type=pl.DeviceIdType.MESH,
    )


def device_of(offset):
    g, w = lax.axis_index("grp"), lax.axis_index("wide")
    x = lax.rem(g + offset[0], 4)
    y = lax.rem(w // 8 + offset[1], 4)
    z = lax.rem(lax.rem(w // 2, 4) + offset[2], 4)
    c = lax.rem(lax.rem(w, 2) + offset[3], 2)
    return x, (y * 4 + z) * 2 + c


def lane():
    return lax.broadcasted_iota(jnp.int32, (8, 128), 1)


def sub():
    return lax.broadcasted_iota(jnp.int32, (8, 128), 0)


def rot(v, shift):
    return pltpu.roll(v, shift % 128, 1)


def turn(v, shift):
    return pltpu.roll(v, shift % 8, 0)


def potential(density):
    return 1.0 - jnp.exp(-density)


def moments(state):
    density = state[0]
    momentum = [None, None, None]
    for d in range(1, 19):
        density = density + state[d]
        for a in range(3):
            c = VELOCITIES[d][a]
            if c:
                m = momentum[a]
                momentum[a] = c * state[d] if m is None else (m + state[d] if c > 0 else m - state[d])
    return [density] + momentum


def relax(density, velocity, states, keep, gain):
    base = 1.0 - 1.5 * (velocity[0] * velocity[0] + velocity[1] * velocity[1] + velocity[2] * velocity[2])
    scaled = {w: (gain * w) * density for w in set(WEIGHTS[d] for d, _ in states)}
    entries = []
    for d, h in states:
        along = None
        for a in range(3):
            c = VELOCITIES[d][a]
            if c:
                term = velocity[a] if c > 0 else -velocity[a]
                along = term if along is None else along + term
        shape = base if along is None else base + along * (3.0 + 4.5 * along)
        entries.append(keep * h + scaled[WEIGHTS[d]] * shape)
    return entries


def collide(mom, pot, grad, states, tau, flip=None):
    inverse = 1.0 / mom[0]
    push = (-tau * COUPLING) * pot
    velocity = [(mom[1 + a] + push * grad[a]) * inverse for a in range(3)]
    if flip is not None:
        velocity[0] = velocity[0] * flip
    return relax(mom[0], velocity, states, 1.0 - 1.0 / tau, 1.0 / tau)


def fine_y(tiles, step, ghost):
    e = lane() & 15
    out = [None] * 8
    edge, inner, outer = (15, 0, 1) if step > 0 else (0, 1, 0)
    for r in range(4):
        across = rot(tiles[outer * 4 + r], 15 * step)
        out[inner * 4 + r] = jnp.where(e == edge, across, rot(tiles[inner * 4 + r], -step))
        out[outer * 4 + r] = jnp.where(e == edge, ghost[r], rot(tiles[outer * 4 + r], -step))
    return out


def fine_z(tiles, step):
    c = lane() >> 4
    moved = [rot(t, -16 * step) for t in tiles]
    edge = 7 if step > 0 else 0
    return [jnp.where(c == edge, moved[j ^ 1], moved[j]) for j in range(len(tiles))]


def fine_x(tiles, step, rows):
    s = sub()
    out = [None] * 8
    for k in range(2):
        for h in range(2):
            low, high = k * 4 + h, k * 4 + 2 + h
            if step > 0:
                out[low] = tiles[high]
                out[high] = jnp.where(s == 7, rows(4 + k * 2 + h), turn(tiles[low], -1))
            else:
                out[high] = tiles[low]
                out[low] = jnp.where(s == 0, rows(k * 2 + h), turn(tiles[high], 1))
    return out


def side_y(tile, step, ghost):
    e, k = lane() & 15, (sub() >> 1) & 1
    edge, inner = (15, 0) if step > 0 else (0, 1)
    across = turn(rot(tile, 15 * step), -2 * step)
    return jnp.where(e == edge, jnp.where(k == inner, across, ghost), rot(tile, -step))


def side_z(tile, step):
    c, h = lane() >> 4, sub() & 1
    moved = rot(tile, -16 * step)
    other = jnp.where(h == 0, turn(moved, -1), turn(moved, 1))
    return jnp.where(c == (7 if step > 0 else 0), other, moved)


def stencil(pot, up, down, back, front):
    total = pot * (1.0 / 18.0) + (up + down + back + front) * (1.0 / 36.0)
    return total, up - down, back - front


def rowcast(row):
    return jnp.broadcast_to(row, (8, 128))


def fine_step(state, mom, ghost_pot, ghost_post, ghost_side, halo, put, work):
    post, tee, face, rows = work
    pots = [mom[4, j] for j in range(8)]
    gp = [ghost_pot[h] for h in range(2)] * 2
    gz = fine_z(gp, 1)
    gz = [a - b for a, b in zip(gz, fine_z(gp, -1))]
    up, down = fine_y(pots, 1, gp), fine_y(pots, -1, gp)
    back, front = fine_z(pots, 1), fine_z(pots, -1)
    parts = [stencil(*v) for v in zip(pots, up, down, back, front)]
    total, dy, dz = ([p[i] for p in parts] for i in range(3))
    zz = [a + b for a, b in zip(fine_z(dy, 1), fine_z(dy, -1))]
    yy = [a + b for a, b in zip(fine_y(dz, 1, gz), fine_y(dz, -1, gz))]
    for j in range(8):
        tee[0, j] = total[j]
        tee[1, j] = dy[j] * (1.0 / 18.0) + zz[j] * (1.0 / 36.0)
        tee[2, j] = dz[j] * (1.0 / 18.0) + yy[j] * (1.0 / 36.0)
        tee[3, j] = dy[j]
        tee[4, j] = dz[j]

    def finish():
        flip = jnp.where(sub() < 4, 1.0, -1.0)
        near, far, own = potential(halo[0]), halo[9], face[...]
        outer, inner = ghost_side[0], ghost_side[1]

        def terms(tile, ghost):
            return stencil(tile, side_y(tile, 1, ghost), side_y(tile, -1, ghost), side_z(tile, 1), side_z(tile, -1))

        t1, y1, z1 = terms(near, outer)
        t2, y2, z2 = terms(far, outer)
        t0, y0, z0 = terms(own, inner)
        goz = side_z(outer, 1) - side_z(outer, -1)
        grad = [
            (t0 - t2) * flip,
            y1 * (1.0 / 18.0) + (y0 + y2 + side_z(y1, 1) + side_z(y1, -1)) * (1.0 / 36.0),
            z1 * (1.0 / 18.0) + (z0 + z2 + side_y(z1, 1, goz) + side_y(z1, -1, goz)) * (1.0 / 36.0),
        ]
        states = [(d, halo[4 + q]) for q, d in enumerate(X_PLUS)]
        for q, v in enumerate(collide([halo[i] for i in range(4)], near, grad, states, FINE_TAU, flip)):
            rows[q] = v
        rows[5], rows[6], rows[7] = t1, y1, z1

        def row(i):
            return lambda r: rowcast(rows[i, r : r + 1, :])

        total, dy, dz = ([tee[i, j] for j in range(8)] for i in (0, 3, 4))
        gx = [a - b for a, b in zip(fine_x(total, 1, row(5)), fine_x(total, -1, row(5)))]
        xy = [a + b for a, b in zip(fine_x(dy, 1, row(6)), fine_x(dy, -1, row(6)))]
        xz = [a + b for a, b in zip(fine_x(dz, 1, row(7)), fine_x(dz, -1, row(7)))]
        for j in range(8):
            tee[0, j] = gx[j]
            tee[1, j] = tee[1, j] + xy[j] * (1.0 / 36.0)
            tee[2, j] = tee[2, j] + xz[j] * (1.0 / 36.0)

        def body(j, _):
            values = collide(
                [mom[i, j] for i in range(4)],
                mom[4, j],
                [tee[i, j] for i in range(3)],
                [(d, state[d, j]) for d in range(19)],
                FINE_TAU,
            )
            for d in range(19):
                post[d, j] = values[d]
            return 0

        lax.fori_loop(0, 8, body, 0)
        for d in range(19):
            tiles = [post[d, j] for j in range(8)]
            cx, cy, cz = VELOCITIES[d]
            if cx:
                tiles = fine_x(tiles, -cx, row((X_PLUS if cx > 0 else X_MINUS).index(d)))
            if cz:
                tiles = fine_z(tiles, -cz)
            if cy:
                q = (Y_PLUS if cy > 0 else Y_MINUS).index(d)
                tiles = fine_y(tiles, -cy, [ghost_post[q, r] for r in range(4)])
            put(d, tiles)

    return finish


def fine_moments(state, mom):
    def body(j, _):
        values = moments([state[d, j] for d in range(19)])
        for i in range(4):
            mom[i, j] = values[i]
        mom[4, j] = potential(values[0])
        return 0

    lax.fori_loop(0, 8, body, 0)


def fine_faces(state, mom, out, face):
    for k in range(2):
        for h in range(2):
            r, low, high = k * 2 + h, k * 4 + h, k * 4 + 2 + h
            for i in range(4):
                out[i, r : r + 1, :] = mom[i, high, 7:8, :]
                out[i, 4 + r : 5 + r, :] = mom[i, low, 0:1, :]
            for q in range(5):
                out[4 + q, r : r + 1, :] = state[X_PLUS[q], high, 7:8, :]
                out[4 + q, 4 + r : 5 + r, :] = state[X_MINUS[q], low, 0:1, :]
            out[9, r : r + 1, :] = mom[4, low, 7:8, :]
            out[9, 4 + r : 5 + r, :] = mom[4, high, 0:1, :]
            face[r : r + 1, :] = mom[4, low, 0:1, :]
            face[4 + r : 5 + r, :] = mom[4, high, 7:8, :]


def kernel(
    fine_hbm, coarse_hbm, slots_hbm, fine_out, coarse_out,
    fine, coarse, slots, si, p1, r1, p2, r2, inv_v, inv_s,
    state, post, mom, tee, face, rows, out1, out2, halo1, halo2,
    layers, low_out, low_in, ghost, edge_r, edge_l, edge_in, ghost_post, ghost_side,
    cmom, face_c, halo_c, rest, rest_out, rest_in, ghost_t, ctee, cpost, cgrad, cedge,
    s1, s2, s3, sg, se, sc, sh1, sh2, sr,
):
    g, w = lax.axis_index("grp"), lax.axis_index("wide")
    me = g * 32 + w
    right, left = lax.rem(g + 1, 4), lax.rem(g + 3, 4)
    ahead, behind = lax.rem(w + 1, 32), lax.rem(w + 31, 32)
    barrier = pltpu.get_barrier_semaphore()
    for offset in OFFSETS:
        pl.semaphore_signal(barrier, inc=1, device_id=device_of(offset), device_id_type=pl.DeviceIdType.MESH)

    loads = [pltpu.make_async_copy(*pair, si.at[i]) for i, pair in enumerate(((fine_hbm, fine), (slots_hbm, slots), (coarse_hbm, coarse)))]
    for load in loads:
        load.start()
    for load in loads:
        load.wait()

    def pack(t, _):
        for k in range(2):
            for q in range(4):
                n = min(5, 19 - 5 * q)
                p1[k, t * 4 + q, 0:n, :] = fine[pl.ds(5 * q * 64 + t * 2 + k, n, stride=64), :]
        return 0

    lax.fori_loop(0, 32, pack, 0)

    place = sub() * 128 + lane()

    def invert(b, acc):
        return jnp.where(place == slots[b], b, acc)

    inv_v[...] = lax.fori_loop(0, 256, invert, jnp.zeros((8, 128), jnp.int32), unroll=8)
    fetch = pltpu.make_async_copy(inv_v, inv_s, s3)
    fetch.start()
    for k in range(2):
        r1[2 * me + k, 0:5, :] = p1[k, me, 0:5, :]

    def coarse_body(i, _):
        values = moments([coarse[d, i] for d in range(19)])
        for a in range(4):
            cmom[a, i + 2] = values[a]
        cmom[4, i + 2] = potential(values[0])
        return 0

    lax.fori_loop(0, 8, coarse_body, 0)
    for q in range(5):
        face_c[0, q] = coarse[X_PLUS[q], 7]
        face_c[1, q] = coarse[X_MINUS[q], 0]
    for a in range(4):
        face_c[0, 5 + a] = cmom[a, 9]
        face_c[1, 5 + a] = cmom[a, 2]
    face_c[0, 9] = cmom[4, 8]
    face_c[1, 9] = cmom[4, 3]

    flat = coarse.reshape(19 * 64, 128)
    e, c_l, s = lane() & 15, lane() >> 4, sub()

    def layer_body(d, _):
        for h in range(2):
            v = None
            for m in range(4):
                t = rot(flat[pl.ds(d * 64 + h * 4 + m, 8, stride=8), :], 32 * m + 15)
                v = t if v is None else jnp.where(c_l >= 2 * m, t, v)
            layers[d, h] = v
        return 0

    lax.fori_loop(0, 19, layer_body, 0)

    def rescaled(source, is_low, factor, h):
        m = moments([source[d, h] for d in range(19)])
        inverse = 1.0 / m[0]
        u = [m[1] * inverse, m[2] * inverse * jnp.where(is_low, 1.0, -1.0), m[3] * inverse]
        states = [(d, jnp.where(is_low, source[d, h], source[Y_MINUS[q], h])) for q, d in enumerate(Y_PLUS)]
        return relax(m[0], u, states, factor, 1.0 - factor) + [potential(m[0])]

    for h in range(2):
        for q, v in enumerate(rescaled(layers, e == 14, TO_FINE, h)):
            low_out[q, h] = jnp.where((c_l & 1) == 1, rot(v, 16), v)

    pl.semaphore_wait(barrier, len(OFFSETS))
    to_ahead = send(low_out, low_in, sg, (g, ahead))
    to_ahead.start()
    for offset in OFFSETS:
        x, y = device_of(offset)
        send(p1.at[:, x * 32 + y, 0:5, :], r1.at[pl.ds(2 * me, 2), 0:5, :], s1, (x, y)).start()
    cf_r = send(face_c.at[0], halo_c.at[0], sc.at[0], (right, w))
    cf_l = send(face_c.at[1], halo_c.at[1], sc.at[1], (left, w))
    cf_r.start()
    cf_l.start()

    to_ahead.wait_recv()
    for q in range(6):
        for h in range(2):
            v = jnp.where(e == 0, rot(low_in[q, h], -14), low_out[q, h])
            ghost[q, h] = v
            edge_r[q * 2 + h : q * 2 + h + 1, :] = v[7:8]
            edge_l[q * 2 + h : q * 2 + h + 1, :] = v[0:1]
    ge_r = send(edge_r, edge_in.at[0], se.at[0], (right, w))
    ge_l = send(edge_l, edge_in.at[1], se.at[1], (left, w))
    ge_r.start()
    ge_l.start()

    fetch.wait()
    all1 = r1.at[0:254, 0:5, :]
    pltpu.make_async_copy(all1, all1, s1.at[1]).wait()

    for start in range(0, 128, 8):
        group = ([(0, 0, 0, 0)] + OFFSETS)[start : start + 8]
        targets = [device_of(offset) for offset in group]
        owners = [x * 32 + y for x, y in targets]
        found = [[inv_s[m // 64, 2 * lax.rem(m, 64) + k] for k in range(2)] for m in owners]
        pieces = [[r1[b, 0:5, :] for b in pair] for pair in found]
        for m, pair in zip(owners, pieces):
            for k in range(2):
                p2[k, m, 0:5, :] = pair[k]
        for m, pair, offset, device in zip(owners, pieces, group, targets):
            if any(offset):
                send(p2.at[:, m, 0:5, :], r2.at[:, me, 0:5, :], s2, device).start()
            else:
                for k in range(2):
                    r2[k, me, 0:5, :] = pair[k]

    ge_r.wait_recv()
    ge_l.wait_recv()
    for q in range(5):
        v = [ghost[q, h] for h in range(2)]
        cx, _, cz = VELOCITIES[Y_PLUS[q]]
        if cz:
            v = fine_z(v, -cz)
        for h in range(2):
            low = high = v[h]
            if cx > 0:
                low = jnp.where(s == 0, rowcast(edge_in[0, q * 2 + h : q * 2 + h + 1, :]), turn(v[h], 1))
            if cx < 0:
                high = jnp.where(s == 7, rowcast(edge_in[1, q * 2 + h : q * 2 + h + 1, :]), turn(v[h], -1))
            ghost_post[q, h] = low
            ghost_post[q, 2 + h] = high
    for k in range(2):
        for h in range(2):
            r = k * 2 + h
            ghost_side[0, r : r + 1, :] = edge_in[0, 10 + h : 11 + h, :]
            ghost_side[0, 4 + r : 5 + r, :] = edge_in[1, 10 + h : 11 + h, :]
            ghost_side[1, r : r + 1, :] = ghost[5, h, 0:1, :]
            ghost_side[1, 4 + r : 5 + r, :] = ghost[5, h, 7:8, :]
    cf_r.wait_recv()
    cf_l.wait_recv()
    for side, (near, far) in enumerate(((1, 0), (10, 11))):
        for a in range(4):
            cmom[a, near] = halo_c[side, 5 + a]
        cmom[4, near] = potential(halo_c[side, 5])
        cmom[4, far] = halo_c[side, 9]

    def coarse_y(v, step):
        return jnp.where(lane() == (127 if step > 0 else 0), 0.0, rot(v, -step))

    def terms_body(i, _):
        v = cmom[4, i]
        t, dy, dz = stencil(v, coarse_y(v, 1), coarse_y(v, -1), turn(v, -1), turn(v, 1))
        ctee[0, i], ctee[1, i], ctee[2, i] = t, dy, dz
        return 0

    lax.fori_loop(0, 12, terms_body, 0)

    def coarse_post(i, states):
        dy, dz = ctee[1, i], ctee[2, i]
        grad = [
            ctee[0, i + 1] - ctee[0, i - 1],
            dy * (1.0 / 18.0) + (ctee[1, i + 1] + ctee[1, i - 1] + turn(dy, 1) + turn(dy, -1)) * (1.0 / 36.0),
            dz * (1.0 / 18.0) + (ctee[2, i + 1] + ctee[2, i - 1] + coarse_y(dz, 1) + coarse_y(dz, -1)) * (1.0 / 36.0),
        ]
        for a in range(3):
            cgrad[a, i] = grad[a]
        values = collide([cmom[a, i] for a in range(4)], cmom[4, i], grad, states, COARSE_TAU)
        for (d, _), v in zip(states, values):
            cpost[d, i] = v

    def post_body(i, _):
        coarse_post(i + 2, [(d, coarse[d, i]) for d in range(19)])
        return 0

    lax.fori_loop(0, 8, post_body, 0)
    coarse_post(1, [(d, halo_c[0, q]) for q, d in enumerate(X_PLUS)])
    coarse_post(10, [(d, halo_c[1, q]) for q, d in enumerate(X_MINUS)])

    def stream_body(i, _):
        for d in range(19):
            cx, cy, cz = VELOCITIES[d]
            v = cpost[d, i + 2 - cx]
            if cz:
                v = turn(v, cz)
            if cy:
                v = rot(v, cy)
            coarse_out[d, i] = v
        return 0

    lax.fori_loop(0, 8, stream_body, 0)

    def packed(load, count):
        v = None
        for i in count:
            t = rot(load(i), 2 * i + 1)
            v = t if v is None else jnp.where(lane() >= 2 * i, t, v)
        return v

    def edge_body(d, _):
        cedge[d] = packed(lambda i: coarse[d, i - 2], range(2, 10))
        return 0

    lax.fori_loop(0, 19, edge_body, 0)
    for side, (dirs, i) in enumerate(((X_PLUS, 1), (X_MINUS, 10))):
        for q, d in enumerate(dirs):
            cedge[d] = jnp.where((lane() >> 1) == i, rot(halo_c[side, q], 2 * i + 1), cedge[d])
    for a in range(5):
        cedge[19 + a] = packed(lambda i: cmom[a, i], range(1, 11))
    for a in range(3):
        cedge[24 + a] = packed(lambda i: cgrad[a, i], range(1, 11))

    all2 = r2.at[:, 0:127, 0:5, :]
    pltpu.make_async_copy(all2, all2, s2.at[1]).wait()
    got = r2.reshape(2048, 128)
    for d in range(19):
        for k in range(2):
            for r in range(4):
                state[d, k * 4 + r] = got[pl.ds(((k * 128 + r * 4 + d // 5) * 8) + d % 5, 8, stride=128), :]

    fine_moments(state, mom)
    fine_faces(state, mom, out1, face)
    f1r = send(out1.at[:, 0:4], halo1.at[:, 0:4], sh1.at[0], (right, w))
    f1l = send(out1.at[:, 4:8], halo1.at[:, 4:8], sh1.at[1], (left, w))
    f1r.start()
    f1l.start()

    for d in range(19):
        for h in range(2):
            v = jnp.where(e < 8, state[d, h] + state[d, 2 + h], state[d, 4 + h] + state[d, 6 + h])
            v = v + rot(v, -1)
            rest[d, h] = 0.125 * (v + rot(v, -16))
    slot = lane() & 31
    for h in range(2):
        tile = jnp.zeros((8, 128), jnp.float32)
        for q, v in enumerate(rescaled(rest, e == 14, TO_COARSE, h)):
            tile = jnp.where(slot == 2 * q, rot(v, 2 * q), jnp.where(slot == 2 * q + 1, rot(v, 2 * q - 13), tile))
        rest_out[h] = tile
    rests = [
        send(rest_out, rest_in.at[i], sr.at[i], device)
        for i, device in enumerate(((g, behind), (right, w), (right, behind), (left, w), (left, behind)))
    ]
    for copy in rests:
        copy.start()

    work = (post, tee, face, rows)

    def keep(d, tiles):
        for j in range(8):
            state[d, j] = tiles[j]

    def give(d, tiles):
        for k in range(2):
            for r in range(4):
                fine_out[pl.ds(d * 64 + r * 2 + k, 8, stride=8), :] = tiles[k * 4 + r]

    ghost_pot = [ghost[5, h] for h in range(2)]
    finish = fine_step(state, mom, ghost_pot, ghost_post, ghost_side, halo1, keep, work)
    f1r.wait_recv()
    f1l.wait_recv()
    finish()
    fine_moments(state, mom)
    fine_faces(state, mom, out2, face)
    f2r = send(out2.at[:, 0:4], halo2.at[:, 0:4], sh2.at[0], (right, w))
    f2l = send(out2.at[:, 4:8], halo2.at[:, 4:8], sh2.at[1], (left, w))
    f2r.start()
    f2l.start()

    for copy in rests:
        copy.wait_recv()
    turned = ghost_t.reshape(192, 128)
    is_low = (lane() & 1) == 1
    for b, (low, high) in enumerate(((rest_out, rest_in.at[0]), (rest_in.at[1], rest_in.at[2]), (rest_in.at[3], rest_in.at[4]))):
        for h in range(2):
            v = jnp.where(is_low, low[h], high[h])
            for m in range(4):
                ghost_t[b, h * 4 + m] = rot(v, -32 * m)
    starts = [64 + 6, 64 + 7] + list(range(8)) + [128, 129]
    columns = [turned[pl.ds(r, 8, stride=8), :] for r in starts]
    entering = []
    for q in range(6):
        v = rot(columns[0], -2 * q)
        for i in range(1, 12):
            v = jnp.where(lane() >= 2 * i, rot(columns[i], 2 * i - 2 * q), v)
        entering.append(v)

    pg = entering[5]
    x_up, x_down, z_up, z_down = rot(pg, -2), rot(pg, 2), turn(pg, -1), turn(pg, 1)
    outward = pg * (1.0 / 18.0) + (x_up + x_down + z_up + z_down) * (1.0 / 36.0)
    grad = [
        cedge[24] + (x_up - x_down) * (1.0 / 36.0),
        cedge[25] + jnp.where(is_low, -outward, outward),
        cedge[26] + (z_up - z_down) * (1.0 / 36.0),
    ]
    again = collide(
        [cedge[19 + a] for a in range(4)], cedge[23], grad, [(d, cedge[d]) for d in range(19)], COARSE_TAU
    )
    for d in range(19):
        cx, cy, cz = VELOCITIES[d]
        v = again[d]
        if cy > 0:
            v, base, mask = jnp.where(is_low, v, rot(entering[Y_PLUS.index(d)], -1)), 0, lane() < 2
        elif cy < 0:
            v, base, mask = jnp.where(is_low, rot(entering[Y_MINUS.index(d)], 1), v), 126, lane() >= 126
        else:
            base, mask = 127, (lane() == 0) | (lane() == 127)
        if cz:
            v = turn(v, cz)
        for x in range(8):
            coarse_out[d, x] = jnp.where(mask, rot(v, base - 2 * (x + 2 - cx)), coarse_out[d, x])

    finish = fine_step(state, mom, ghost_pot, ghost_post, ghost_side, halo2, give, work)
    f2r.wait_recv()
    f2l.wait_recv()
    finish()
    for copy in (to_ahead, ge_r, ge_l, cf_r, cf_l, f1r, f1l, f2r, f2l, *rests):
        copy.wait_send()
    pltpu.make_async_copy(all1, all1, s1.at[0]).wait()
    pltpu.make_async_copy(all2, all2, s2.at[0]).wait()


def local(fine_pop, coarse_pop, new_slot):
    def tiles(*shape):
        return pltpu.VMEM(shape + (8, 128), jnp.float32)

    def sems(*shape):
        return pltpu.SemaphoreType.DMA(shape)

    vmem = pl.BlockSpec(memory_space=pltpu.VMEM)
    fine_out, coarse_out = pl.pallas_call(
        kernel,
        out_shape=(
            jax.ShapeDtypeStruct((1216, 128), jnp.float32),
            jax.ShapeDtypeStruct((19, 8, 8, 128), jnp.float32),
        ),
        in_specs=[pl.BlockSpec(memory_space=pltpu.HBM)] * 3,
        out_specs=(vmem, vmem),
        scratch_shapes=[
            pltpu.VMEM((1216, 128), jnp.float32), tiles(19, 8), pltpu.SMEM((256,), jnp.int32), sems(3),
            tiles(2, 128), tiles(256), tiles(2, 128), tiles(2, 128),
            pltpu.VMEM((8, 128), jnp.int32), pltpu.SMEM((8, 128), jnp.int32),
            tiles(19, 8), tiles(19, 8), tiles(5, 8), tiles(5, 8), tiles(), tiles(8),
            tiles(10), tiles(10), tiles(10), tiles(10),
            tiles(19, 2), tiles(6, 2), tiles(6, 2), tiles(6, 2),
            pltpu.VMEM((12, 128), jnp.float32), pltpu.VMEM((12, 128), jnp.float32),
            pltpu.VMEM((2, 12, 128), jnp.float32), tiles(5, 4), tiles(2),
            tiles(5, 12), tiles(2, 10), tiles(2, 10), tiles(19, 2), tiles(2), tiles(5, 2),
            tiles(3, 8), tiles(3, 12), tiles(19, 12), tiles(3, 12), tiles(27),
            sems(2), sems(2), pltpu.SemaphoreType.DMA, sems(2), sems(2, 2), sems(2, 2),
            sems(2, 2), sems(2, 2), sems(5, 2),
        ],
        compiler_params=pltpu.CompilerParams(
            collective_id=0, has_side_effects=True, vmem_limit_bytes=53836 * 1024
        ),
    )(fine_pop.reshape(2, 19, 32, 128).transpose(1, 2, 0, 3).reshape(1216, 128), coarse_pop, new_slot)
    fine_out = fine_out.reshape(19, 32, 2, 128).transpose(2, 0, 1, 3).reshape(2, 19, 4096)
    return fine_out, coarse_out


def solution(mesh):
    return jax.shard_map(
        local,
        mesh=mesh,
        in_specs=(P(("grp", "wide"), None, None), P(None, "grp", None, "wide"), P()),
        out_specs=(P(("grp", "wide"), None, None), P(None, "grp", None, "wide")),
        check_vma=False,
    )
```

```python
import jax
import jax.numpy as jnp
from jax import lax
from jax.experimental import pallas as pl
from jax.experimental.pallas import tpu as pltpu
from jax.sharding import PartitionSpec as P

VELOCITIES = (
    (0, 0, 0),
    (1, 0, 0),
    (-1, 0, 0),
    (0, 1, 0),
    (0, -1, 0),
    (0, 0, 1),
    (0, 0, -1),
    (1, 1, 0),
    (-1, -1, 0),
    (1, -1, 0),
    (-1, 1, 0),
    (1, 0, 1),
    (-1, 0, -1),
    (1, 0, -1),
    (-1, 0, 1),
    (0, 1, 1),
    (0, -1, -1),
    (0, 1, -1),
    (0, -1, 1),
)
WEIGHTS = (1.0 / 3.0,) + (1.0 / 18.0,) * 6 + (1.0 / 36.0,) * 12
COUPLING = -5.0
FINE_TAU = 1.1
COARSE_TAU = 0.8
TO_COARSE = 2.0 * COARSE_TAU / FINE_TAU
TO_FINE = FINE_TAU / (2.0 * COARSE_TAU)

INDEX = {c: i for i, c in enumerate(VELOCITIES)}
X_PLUS = (1, 7, 9, 11, 13)
X_MINUS = tuple(INDEX[(-c[0], c[1], c[2])] for c in (VELOCITIES[i] for i in X_PLUS))
Y_PLUS = (3, 7, 10, 15, 17)
Y_MINUS = tuple(INDEX[(c[0], -c[1], c[2])] for c in (VELOCITIES[i] for i in Y_PLUS))

PARTS = ((0, 1), (1, 2), (2, 5))
OFFSETS = sorted(
    ((a, b, c, d) for a in range(4) for b in range(4) for c in range(4) for d in range(2) if a + b + c + d),
    key=lambda o: (-sum(min(v, 4 - v) for v in o[:3]), (o[0] * 7 + o[1] * 5 + o[2] * 3 + o[3]) % 11),
)


def send(src, dst, sems, device):
    return pltpu.make_async_remote_copy(
        src_ref=src,
        dst_ref=dst,
        send_sem=sems.at[0],
        recv_sem=sems.at[1],
        device_id=device,
        device_id_type=pl.DeviceIdType.MESH,
    )


def device_of(offset):
    g, w = lax.axis_index("grp"), lax.axis_index("wide")
    x = lax.rem(g + offset[0], 4)
    y = lax.rem(w // 8 + offset[1], 4)
    z = lax.rem(lax.rem(w // 2, 4) + offset[2], 4)
    c = lax.rem(lax.rem(w, 2) + offset[3], 2)
    return x, (y * 4 + z) * 2 + c


def lane():
    return lax.broadcasted_iota(jnp.int32, (8, 128), 1)


def sub():
    return lax.broadcasted_iota(jnp.int32, (8, 128), 0)


def rot(v, shift):
    return pltpu.roll(v, shift % 128, 1)


def turn(v, shift):
    return pltpu.roll(v, shift % 8, 0)


def potential(density):
    return 1.0 - jnp.exp(-density)


def moments(state):
    density = state[0]
    momentum = [None, None, None]
    for d in range(1, 19):
        density = density + state[d]
        for a in range(3):
            c = VELOCITIES[d][a]
            if c:
                m = momentum[a]
                momentum[a] = c * state[d] if m is None else (m + state[d] if c > 0 else m - state[d])
    return [density] + momentum


def relax(density, velocity, states, keep, gain):
    base = 1.0 - 1.5 * (velocity[0] * velocity[0] + velocity[1] * velocity[1] + velocity[2] * velocity[2])
    scaled = {w: (gain * w) * density for w in set(WEIGHTS[d] for d, _ in states)}
    entries = []
    for d, h in states:
        along = None
        for a in range(3):
            c = VELOCITIES[d][a]
            if c:
                term = velocity[a] if c > 0 else -velocity[a]
                along = term if along is None else along + term
        shape = base if along is None else base + along * (3.0 + 4.5 * along)
        entries.append(keep * h + scaled[WEIGHTS[d]] * shape)
    return entries


def collide(mom, pot, grad, states, tau, flip=None):
    inverse = 1.0 / mom[0]
    push = (-tau * COUPLING) * pot
    velocity = [(mom[1 + a] + push * grad[a]) * inverse for a in range(3)]
    if flip is not None:
        velocity[0] = velocity[0] * flip
    return relax(mom[0], velocity, states, 1.0 - 1.0 / tau, 1.0 / tau)


def fine_y(tiles, step, ghost):
    e = lane() & 15
    out = [None] * 8
    edge, inner, outer = (15, 0, 1) if step > 0 else (0, 1, 0)
    for r in range(4):
        across = rot(tiles[outer * 4 + r], 15 * step)
        out[inner * 4 + r] = jnp.where(e == edge, across, rot(tiles[inner * 4 + r], -step))
        out[outer * 4 + r] = jnp.where(e == edge, ghost[r], rot(tiles[outer * 4 + r], -step))
    return out


def fine_z(tiles, step):
    c = lane() >> 4
    moved = [rot(t, -16 * step) for t in tiles]
    edge = 7 if step > 0 else 0
    return [jnp.where(c == edge, moved[j ^ 1], moved[j]) for j in range(len(tiles))]


def fine_x(tiles, step, rows):
    s = sub()
    out = [None] * 8
    for k in range(2):
        for h in range(2):
            low, high = k * 4 + h, k * 4 + 2 + h
            if step > 0:
                out[low] = tiles[high]
                out[high] = jnp.where(s == 7, rows(4 + k * 2 + h), turn(tiles[low], -1))
            else:
                out[high] = tiles[low]
                out[low] = jnp.where(s == 0, rows(k * 2 + h), turn(tiles[high], 1))
    return out


def side_y(tile, step, ghost):
    e, k = lane() & 15, (sub() >> 1) & 1
    edge, inner = (15, 0) if step > 0 else (0, 1)
    across = turn(rot(tile, 15 * step), -2 * step)
    return jnp.where(e == edge, jnp.where(k == inner, across, ghost), rot(tile, -step))


def side_z(tile, step):
    c, h = lane() >> 4, sub() & 1
    moved = rot(tile, -16 * step)
    other = jnp.where(h == 0, turn(moved, -1), turn(moved, 1))
    return jnp.where(c == (7 if step > 0 else 0), other, moved)


def stencil(pot, up, down, back, front):
    total = pot * (1.0 / 18.0) + (up + down + back + front) * (1.0 / 36.0)
    return total, up - down, back - front


def rowcast(row):
    return jnp.broadcast_to(row, (8, 128))


def fine_step(state, mom, ghost_pot, ghost_post, ghost_side, halo, put, work):
    post, tee, face, rows = work
    pots = [mom[4, j] for j in range(8)]
    gp = [ghost_pot[h] for h in range(2)] * 2
    gz = fine_z(gp, 1)
    gz = [a - b for a, b in zip(gz, fine_z(gp, -1))]
    up, down = fine_y(pots, 1, gp), fine_y(pots, -1, gp)
    back, front = fine_z(pots, 1), fine_z(pots, -1)
    parts = [stencil(*v) for v in zip(pots, up, down, back, front)]
    total, dy, dz = ([p[i] for p in parts] for i in range(3))
    zz = [a + b for a, b in zip(fine_z(dy, 1), fine_z(dy, -1))]
    yy = [a + b for a, b in zip(fine_y(dz, 1, gz), fine_y(dz, -1, gz))]
    for j in range(8):
        tee[0, j] = total[j]
        tee[1, j] = dy[j] * (1.0 / 18.0) + zz[j] * (1.0 / 36.0)
        tee[2, j] = dz[j] * (1.0 / 18.0) + yy[j] * (1.0 / 36.0)
        tee[3, j] = dy[j]
        tee[4, j] = dz[j]

    def finish():
        flip = jnp.where(sub() < 4, 1.0, -1.0)
        near, far, own = potential(halo[0]), halo[9], face[...]
        outer, inner = ghost_side[0], ghost_side[1]

        def terms(tile, ghost):
            return stencil(tile, side_y(tile, 1, ghost), side_y(tile, -1, ghost), side_z(tile, 1), side_z(tile, -1))

        t1, y1, z1 = terms(near, outer)
        t2, y2, z2 = terms(far, outer)
        t0, y0, z0 = terms(own, inner)
        goz = side_z(outer, 1) - side_z(outer, -1)
        grad = [
            (t0 - t2) * flip,
            y1 * (1.0 / 18.0) + (y0 + y2 + side_z(y1, 1) + side_z(y1, -1)) * (1.0 / 36.0),
            z1 * (1.0 / 18.0) + (z0 + z2 + side_y(z1, 1, goz) + side_y(z1, -1, goz)) * (1.0 / 36.0),
        ]
        states = [(d, halo[4 + q]) for q, d in enumerate(X_PLUS)]
        for q, v in enumerate(collide([halo[i] for i in range(4)], near, grad, states, FINE_TAU, flip)):
            rows[q] = v
        rows[5], rows[6], rows[7] = t1, y1, z1

        def row(i):
            return lambda r: rowcast(rows[i, r : r + 1, :])

        total, dy, dz = ([tee[i, j] for j in range(8)] for i in (0, 3, 4))
        gx = [a - b for a, b in zip(fine_x(total, 1, row(5)), fine_x(total, -1, row(5)))]
        xy = [a + b for a, b in zip(fine_x(dy, 1, row(6)), fine_x(dy, -1, row(6)))]
        xz = [a + b for a, b in zip(fine_x(dz, 1, row(7)), fine_x(dz, -1, row(7)))]
        for j in range(8):
            tee[0, j] = gx[j]
            tee[1, j] = tee[1, j] + xy[j] * (1.0 / 36.0)
            tee[2, j] = tee[2, j] + xz[j] * (1.0 / 36.0)

        def body(j, _):
            values = collide(
                [mom[i, j] for i in range(4)],
                mom[4, j],
                [tee[i, j] for i in range(3)],
                [(d, state[d, j]) for d in range(19)],
                FINE_TAU,
            )
            for d in range(19):
                post[d, j] = values[d]
            return 0

        lax.fori_loop(0, 8, body, 0)
        for d in range(19):
            tiles = [post[d, j] for j in range(8)]
            cx, cy, cz = VELOCITIES[d]
            if cx:
                tiles = fine_x(tiles, -cx, row((X_PLUS if cx > 0 else X_MINUS).index(d)))
            if cz:
                tiles = fine_z(tiles, -cz)
            if cy:
                q = (Y_PLUS if cy > 0 else Y_MINUS).index(d)
                tiles = fine_y(tiles, -cy, [ghost_post[q, r] for r in range(4)])
            put(d, tiles)

    return finish


def fine_moments(state, mom):
    def body(j, _):
        values = moments([state[d, j] for d in range(19)])
        for i in range(4):
            mom[i, j] = values[i]
        mom[4, j] = potential(values[0])
        return 0

    lax.fori_loop(0, 8, body, 0)


def fine_faces(state, mom, out, face):
    for k in range(2):
        for h in range(2):
            r, low, high = k * 2 + h, k * 4 + h, k * 4 + 2 + h
            for i in range(4):
                out[i, r : r + 1, :] = mom[i, high, 7:8, :]
                out[i, 4 + r : 5 + r, :] = mom[i, low, 0:1, :]
            for q in range(5):
                out[4 + q, r : r + 1, :] = state[X_PLUS[q], high, 7:8, :]
                out[4 + q, 4 + r : 5 + r, :] = state[X_MINUS[q], low, 0:1, :]
            out[9, r : r + 1, :] = mom[4, low, 7:8, :]
            out[9, 4 + r : 5 + r, :] = mom[4, high, 0:1, :]
            face[r : r + 1, :] = mom[4, low, 0:1, :]
            face[4 + r : 5 + r, :] = mom[4, high, 7:8, :]


def kernel(
    fine_hbm, coarse_hbm, slots_hbm, fine_out, coarse_out,
    fine, coarse, slots, si, p1, r1_0, r1_1, r1_2, p2, r2, inv_v, inv_s,
    state, post, mom, tee, face, rows, out1, out2, halo1, halo2,
    layers, low_out, low_in, ghost, edge_r, edge_l, edge_in, ghost_post, ghost_side,
    cmom, face_c, halo_c, rest, rest_out, rest_in, ghost_t, ctee, cpost, cgrad, cedge,
    s1, s2, s3, sg, se, sc, sh1, sh2, sr,
):
    g, w = lax.axis_index("grp"), lax.axis_index("wide")
    me = g * 32 + w
    right, left = lax.rem(g + 1, 4), lax.rem(g + 3, 4)
    ahead, behind = lax.rem(w + 1, 32), lax.rem(w + 31, 32)
    barrier = pltpu.get_barrier_semaphore()
    r1 = (r1_0, r1_1, r1_2)
    for offset in OFFSETS:
        pl.semaphore_signal(barrier, inc=1, device_id=device_of(offset), device_id_type=pl.DeviceIdType.MESH)

    loads = [pltpu.make_async_copy(*pair, si.at[i]) for i, pair in enumerate(((fine_hbm, fine), (slots_hbm, slots), (coarse_hbm, coarse)))]
    for load in loads:
        load.start()
    for load in loads:
        load.wait()

    def pack(t, _):
        for k in range(2):
            for q in range(4):
                n = min(5, 19 - 5 * q)
                p1[k, t * 4 + q, 0:n, :] = fine[pl.ds(5 * q * 64 + t * 2 + k, n, stride=64), :]
        return 0

    lax.fori_loop(0, 32, pack, 0)

    place = sub() * 128 + lane()

    def invert(b, acc):
        return jnp.where(place == slots[b], b, acc)

    inv_v[...] = lax.fori_loop(0, 256, invert, jnp.zeros((8, 128), jnp.int32), unroll=8)
    fetch = pltpu.make_async_copy(inv_v, inv_s, s3)
    fetch.start()
    for k in range(2):
        for part, (lo, hi) in enumerate(PARTS):
            r1[part][2 * me + k, lo:hi, :] = p1[k, me, lo:hi, :]

    def coarse_body(i, _):
        values = moments([coarse[d, i] for d in range(19)])
        for a in range(4):
            cmom[a, i + 2] = values[a]
        cmom[4, i + 2] = potential(values[0])
        return 0

    lax.fori_loop(0, 8, coarse_body, 0)
    for q in range(5):
        face_c[0, q] = coarse[X_PLUS[q], 7]
        face_c[1, q] = coarse[X_MINUS[q], 0]
    for a in range(4):
        face_c[0, 5 + a] = cmom[a, 9]
        face_c[1, 5 + a] = cmom[a, 2]
    face_c[0, 9] = cmom[4, 8]
    face_c[1, 9] = cmom[4, 3]

    flat = coarse.reshape(19 * 64, 128)
    e, c_l, s = lane() & 15, lane() >> 4, sub()

    def layer_body(d, _):
        for h in range(2):
            v = None
            for m in range(4):
                t = rot(flat[pl.ds(d * 64 + h * 4 + m, 8, stride=8), :], 32 * m + 15)
                v = t if v is None else jnp.where(c_l >= 2 * m, t, v)
            layers[d, h] = v
        return 0

    lax.fori_loop(0, 19, layer_body, 0)

    def rescaled(source, is_low, factor, h):
        m = moments([source[d, h] for d in range(19)])
        inverse = 1.0 / m[0]
        u = [m[1] * inverse, m[2] * inverse * jnp.where(is_low, 1.0, -1.0), m[3] * inverse]
        states = [(d, jnp.where(is_low, source[d, h], source[Y_MINUS[q], h])) for q, d in enumerate(Y_PLUS)]
        return relax(m[0], u, states, factor, 1.0 - factor) + [potential(m[0])]

    for h in range(2):
        for q, v in enumerate(rescaled(layers, e == 14, TO_FINE, h)):
            low_out[q, h] = jnp.where((c_l & 1) == 1, rot(v, 16), v)

    pl.semaphore_wait(barrier, len(OFFSETS))
    to_ahead = send(low_out, low_in, sg, (g, ahead))
    to_ahead.start()
    for part, (lo, hi) in enumerate(PARTS):
        for offset in OFFSETS:
            x, y = device_of(offset)
            send(p1.at[:, x * 32 + y, lo:hi, :], r1[part].at[pl.ds(2 * me, 2), lo:hi, :], s1.at[part], (x, y)).start()
    cf_r = send(face_c.at[0], halo_c.at[0], sc.at[0], (right, w))
    cf_l = send(face_c.at[1], halo_c.at[1], sc.at[1], (left, w))
    cf_r.start()
    cf_l.start()

    to_ahead.wait_recv()
    for q in range(6):
        for h in range(2):
            v = jnp.where(e == 0, rot(low_in[q, h], -14), low_out[q, h])
            ghost[q, h] = v
            edge_r[q * 2 + h : q * 2 + h + 1, :] = v[7:8]
            edge_l[q * 2 + h : q * 2 + h + 1, :] = v[0:1]
    ge_r = send(edge_r, edge_in.at[0], se.at[0], (right, w))
    ge_l = send(edge_l, edge_in.at[1], se.at[1], (left, w))
    ge_r.start()
    ge_l.start()

    fetch.wait()

    everyone = [(0, 0, 0, 0)] + OFFSETS
    for part, (lo, hi) in enumerate(PARTS):
        arrived = r1[part].at[0:254, lo:hi, :]
        pltpu.make_async_copy(arrived, arrived, s1.at[part, 1]).wait()
        for start in range(0, 128, 8):
            group = everyone[start : start + 8]
            targets = [device_of(offset) for offset in group]
            owners = [x * 32 + y for x, y in targets]
            found = [[inv_s[m // 64, 2 * lax.rem(m, 64) + k] for k in range(2)] for m in owners]
            pieces = [[r1[part][b, lo:hi, :] for b in pair] for pair in found]
            for m, pair in zip(owners, pieces):
                for k in range(2):
                    p2[k, m, lo:hi, :] = pair[k]
            for m, pair, offset, device in zip(owners, pieces, group, targets):
                if any(offset):
                    send(p2.at[:, m, lo:hi, :], r2.at[:, me, lo:hi, :], s2.at[part], device).start()
                else:
                    for k in range(2):
                        r2[k, me, lo:hi, :] = pair[k]

    ge_r.wait_recv()
    ge_l.wait_recv()
    for q in range(5):
        v = [ghost[q, h] for h in range(2)]
        cx, _, cz = VELOCITIES[Y_PLUS[q]]
        if cz:
            v = fine_z(v, -cz)
        for h in range(2):
            low = high = v[h]
            if cx > 0:
                low = jnp.where(s == 0, rowcast(edge_in[0, q * 2 + h : q * 2 + h + 1, :]), turn(v[h], 1))
            if cx < 0:
                high = jnp.where(s == 7, rowcast(edge_in[1, q * 2 + h : q * 2 + h + 1, :]), turn(v[h], -1))
            ghost_post[q, h] = low
            ghost_post[q, 2 + h] = high
    for k in range(2):
        for h in range(2):
            r = k * 2 + h
            ghost_side[0, r : r + 1, :] = edge_in[0, 10 + h : 11 + h, :]
            ghost_side[0, 4 + r : 5 + r, :] = edge_in[1, 10 + h : 11 + h, :]
            ghost_side[1, r : r + 1, :] = ghost[5, h, 0:1, :]
            ghost_side[1, 4 + r : 5 + r, :] = ghost[5, h, 7:8, :]
    cf_r.wait_recv()
    cf_l.wait_recv()
    for side, (near, far) in enumerate(((1, 0), (10, 11))):
        for a in range(4):
            cmom[a, near] = halo_c[side, 5 + a]
        cmom[4, near] = potential(halo_c[side, 5])
        cmom[4, far] = halo_c[side, 9]

    def coarse_y(v, step):
        return jnp.where(lane() == (127 if step > 0 else 0), 0.0, rot(v, -step))

    def terms_body(i, _):
        v = cmom[4, i]
        t, dy, dz = stencil(v, coarse_y(v, 1), coarse_y(v, -1), turn(v, -1), turn(v, 1))
        ctee[0, i], ctee[1, i], ctee[2, i] = t, dy, dz
        return 0

    lax.fori_loop(0, 12, terms_body, 0)

    def coarse_post(i, states):
        dy, dz = ctee[1, i], ctee[2, i]
        grad = [
            ctee[0, i + 1] - ctee[0, i - 1],
            dy * (1.0 / 18.0) + (ctee[1, i + 1] + ctee[1, i - 1] + turn(dy, 1) + turn(dy, -1)) * (1.0 / 36.0),
            dz * (1.0 / 18.0) + (ctee[2, i + 1] + ctee[2, i - 1] + coarse_y(dz, 1) + coarse_y(dz, -1)) * (1.0 / 36.0),
        ]
        for a in range(3):
            cgrad[a, i] = grad[a]
        values = collide([cmom[a, i] for a in range(4)], cmom[4, i], grad, states, COARSE_TAU)
        for (d, _), v in zip(states, values):
            cpost[d, i] = v

    def post_body(i, _):
        coarse_post(i + 2, [(d, coarse[d, i]) for d in range(19)])
        return 0

    lax.fori_loop(0, 8, post_body, 0)
    coarse_post(1, [(d, halo_c[0, q]) for q, d in enumerate(X_PLUS)])
    coarse_post(10, [(d, halo_c[1, q]) for q, d in enumerate(X_MINUS)])

    def stream_body(i, _):
        for d in range(19):
            cx, cy, cz = VELOCITIES[d]
            v = cpost[d, i + 2 - cx]
            if cz:
                v = turn(v, cz)
            if cy:
                v = rot(v, cy)
            coarse_out[d, i] = v
        return 0

    lax.fori_loop(0, 8, stream_body, 0)

    def packed(load, count):
        v = None
        for i in count:
            t = rot(load(i), 2 * i + 1)
            v = t if v is None else jnp.where(lane() >= 2 * i, t, v)
        return v

    def edge_body(d, _):
        cedge[d] = packed(lambda i: coarse[d, i - 2], range(2, 10))
        return 0

    lax.fori_loop(0, 19, edge_body, 0)
    for side, (dirs, i) in enumerate(((X_PLUS, 1), (X_MINUS, 10))):
        for q, d in enumerate(dirs):
            cedge[d] = jnp.where((lane() >> 1) == i, rot(halo_c[side, q], 2 * i + 1), cedge[d])
    for a in range(5):
        cedge[19 + a] = packed(lambda i: cmom[a, i], range(1, 11))
    for a in range(3):
        cedge[24 + a] = packed(lambda i: cgrad[a, i], range(1, 11))

    for part, (lo, hi) in enumerate(PARTS):
        arrived = r2.at[:, 0:127, lo:hi, :]
        pltpu.make_async_copy(arrived, arrived, s2.at[part, 1]).wait()
    got = r2.reshape(2048, 128)
    for d in range(19):
        for k in range(2):
            for r in range(4):
                state[d, k * 4 + r] = got[pl.ds(((k * 128 + r * 4 + d // 5) * 8) + d % 5, 8, stride=128), :]

    fine_moments(state, mom)
    fine_faces(state, mom, out1, face)
    f1r = send(out1.at[:, 0:4], halo1.at[:, 0:4], sh1.at[0], (right, w))
    f1l = send(out1.at[:, 4:8], halo1.at[:, 4:8], sh1.at[1], (left, w))
    f1r.start()
    f1l.start()

    for d in range(19):
        for h in range(2):
            v = jnp.where(e < 8, state[d, h] + state[d, 2 + h], state[d, 4 + h] + state[d, 6 + h])
            v = v + rot(v, -1)
            rest[d, h] = 0.125 * (v + rot(v, -16))
    slot = lane() & 31
    for h in range(2):
        tile = jnp.zeros((8, 128), jnp.float32)
        for q, v in enumerate(rescaled(rest, e == 14, TO_COARSE, h)):
            tile = jnp.where(slot == 2 * q, rot(v, 2 * q), jnp.where(slot == 2 * q + 1, rot(v, 2 * q - 13), tile))
        rest_out[h] = tile
    rests = [
        send(rest_out, rest_in.at[i], sr.at[i], device)
        for i, device in enumerate(((g, behind), (right, w), (right, behind), (left, w), (left, behind)))
    ]
    for copy in rests:
        copy.start()

    work = (post, tee, face, rows)

    def keep(d, tiles):
        for j in range(8):
            state[d, j] = tiles[j]

    def give(d, tiles):
        for k in range(2):
            for r in range(4):
                fine_out[pl.ds(d * 64 + r * 2 + k, 8, stride=8), :] = tiles[k * 4 + r]

    ghost_pot = [ghost[5, h] for h in range(2)]
    finish = fine_step(state, mom, ghost_pot, ghost_post, ghost_side, halo1, keep, work)
    f1r.wait_recv()
    f1l.wait_recv()
    finish()
    fine_moments(state, mom)
    fine_faces(state, mom, out2, face)
    f2r = send(out2.at[:, 0:4], halo2.at[:, 0:4], sh2.at[0], (right, w))
    f2l = send(out2.at[:, 4:8], halo2.at[:, 4:8], sh2.at[1], (left, w))
    f2r.start()
    f2l.start()

    for copy in rests:
        copy.wait_recv()
    turned = ghost_t.reshape(192, 128)
    is_low = (lane() & 1) == 1
    for b, (low, high) in enumerate(((rest_out, rest_in.at[0]), (rest_in.at[1], rest_in.at[2]), (rest_in.at[3], rest_in.at[4]))):
        for h in range(2):
            v = jnp.where(is_low, low[h], high[h])
            for m in range(4):
                ghost_t[b, h * 4 + m] = rot(v, -32 * m)
    starts = [64 + 6, 64 + 7] + list(range(8)) + [128, 129]
    columns = [turned[pl.ds(r, 8, stride=8), :] for r in starts]
    entering = []
    for q in range(6):
        v = rot(columns[0], -2 * q)
        for i in range(1, 12):
            v = jnp.where(lane() >= 2 * i, rot(columns[i], 2 * i - 2 * q), v)
        entering.append(v)

    pg = entering[5]
    x_up, x_down, z_up, z_down = rot(pg, -2), rot(pg, 2), turn(pg, -1), turn(pg, 1)
    outward = pg * (1.0 / 18.0) + (x_up + x_down + z_up + z_down) * (1.0 / 36.0)
    grad = [
        cedge[24] + (x_up - x_down) * (1.0 / 36.0),
        cedge[25] + jnp.where(is_low, -outward, outward),
        cedge[26] + (z_up - z_down) * (1.0 / 36.0),
    ]
    again = collide(
        [cedge[19 + a] for a in range(4)], cedge[23], grad, [(d, cedge[d]) for d in range(19)], COARSE_TAU
    )
    for d in range(19):
        cx, cy, cz = VELOCITIES[d]
        v = again[d]
        if cy > 0:
            v, base, mask = jnp.where(is_low, v, rot(entering[Y_PLUS.index(d)], -1)), 0, lane() < 2
        elif cy < 0:
            v, base, mask = jnp.where(is_low, rot(entering[Y_MINUS.index(d)], 1), v), 126, lane() >= 126
        else:
            base, mask = 127, (lane() == 0) | (lane() == 127)
        if cz:
            v = turn(v, cz)
        for x in range(8):
            coarse_out[d, x] = jnp.where(mask, rot(v, base - 2 * (x + 2 - cx)), coarse_out[d, x])

    finish = fine_step(state, mom, ghost_pot, ghost_post, ghost_side, halo2, give, work)
    f2r.wait_recv()
    f2l.wait_recv()
    finish()
    for copy in (to_ahead, ge_r, ge_l, cf_r, cf_l, f1r, f1l, f2r, f2l, *rests):
        copy.wait_send()
    for part, (lo, hi) in enumerate(PARTS):
        for left_here, sems in ((r1[part].at[0:254, lo:hi, :], s1), (r2.at[:, 0:127, lo:hi, :], s2)):
            pltpu.make_async_copy(left_here, left_here, sems.at[part, 0]).wait()


def local(fine_pop, coarse_pop, new_slot):
    def tiles(*shape):
        return pltpu.VMEM(shape + (8, 128), jnp.float32)

    def sems(*shape):
        return pltpu.SemaphoreType.DMA(shape)

    vmem = pl.BlockSpec(memory_space=pltpu.VMEM)
    fine_out, coarse_out = pl.pallas_call(
        kernel,
        out_shape=(
            jax.ShapeDtypeStruct((1216, 128), jnp.float32),
            jax.ShapeDtypeStruct((19, 8, 8, 128), jnp.float32),
        ),
        in_specs=[pl.BlockSpec(memory_space=pltpu.HBM)] * 3,
        out_specs=(vmem, vmem),
        scratch_shapes=[
            pltpu.VMEM((1216, 128), jnp.float32), tiles(19, 8), pltpu.SMEM((256,), jnp.int32), sems(3),
            tiles(2, 128), tiles(256), tiles(256), tiles(256), tiles(2, 128), tiles(2, 128),
            pltpu.VMEM((8, 128), jnp.int32), pltpu.SMEM((8, 128), jnp.int32),
            tiles(19, 8), tiles(19, 8), tiles(5, 8), tiles(5, 8), tiles(), tiles(8),
            tiles(10), tiles(10), tiles(10), tiles(10),
            tiles(19, 2), tiles(6, 2), tiles(6, 2), tiles(6, 2),
            pltpu.VMEM((12, 128), jnp.float32), pltpu.VMEM((12, 128), jnp.float32),
            pltpu.VMEM((2, 12, 128), jnp.float32), tiles(5, 4), tiles(2),
            tiles(5, 12), tiles(2, 10), tiles(2, 10), tiles(19, 2), tiles(2), tiles(5, 2),
            tiles(3, 8), tiles(3, 12), tiles(19, 12), tiles(3, 12), tiles(27),
            sems(len(PARTS), 2), sems(len(PARTS), 2), pltpu.SemaphoreType.DMA, sems(2), sems(2, 2), sems(2, 2),
            sems(2, 2), sems(2, 2), sems(5, 2),
        ],
        compiler_params=pltpu.CompilerParams(
            collective_id=0, has_side_effects=True, vmem_limit_bytes=53836 * 1024
        ),
    )(fine_pop.reshape(2, 19, 32, 128).transpose(1, 2, 0, 3).reshape(1216, 128), coarse_pop, new_slot)
    fine_out = fine_out.reshape(19, 32, 2, 128).transpose(2, 0, 1, 3).reshape(2, 19, 4096)
    return fine_out, coarse_out


def solution(mesh):
    return jax.shard_map(
        local,
        mesh=mesh,
        in_specs=(P(("grp", "wide"), None, None), P(None, "grp", None, "wide"), P()),
        out_specs=(P(("grp", "wide"), None, None), P(None, "grp", None, "wide")),
        check_vma=False,
    )
```

```python
import jax
import jax.numpy as jnp
from jax import lax
from jax.experimental import pallas as pl
from jax.experimental.pallas import tpu as pltpu
from jax.sharding import PartitionSpec as P

VELOCITIES = (
    (0, 0, 0),
    (1, 0, 0),
    (-1, 0, 0),
    (0, 1, 0),
    (0, -1, 0),
    (0, 0, 1),
    (0, 0, -1),
    (1, 1, 0),
    (-1, -1, 0),
    (1, -1, 0),
    (-1, 1, 0),
    (1, 0, 1),
    (-1, 0, -1),
    (1, 0, -1),
    (-1, 0, 1),
    (0, 1, 1),
    (0, -1, -1),
    (0, 1, -1),
    (0, -1, 1),
)
WEIGHTS = (1.0 / 3.0,) + (1.0 / 18.0,) * 6 + (1.0 / 36.0,) * 12
COUPLING = -5.0
FINE_TAU = 1.1
COARSE_TAU = 0.8
TO_COARSE = 2.0 * COARSE_TAU / FINE_TAU
TO_FINE = FINE_TAU / (2.0 * COARSE_TAU)

INDEX = {c: i for i, c in enumerate(VELOCITIES)}
X_PLUS = (1, 7, 9, 11, 13)
X_MINUS = tuple(INDEX[(-c[0], c[1], c[2])] for c in (VELOCITIES[i] for i in X_PLUS))
Y_PLUS = (3, 7, 10, 15, 17)
Y_MINUS = tuple(INDEX[(c[0], -c[1], c[2])] for c in (VELOCITIES[i] for i in Y_PLUS))

PARTS = ((0, 1), (1, 2), (2, 5))
OFFSETS = sorted(
    ((a, b, c, d) for a in range(4) for b in range(4) for c in range(4) for d in range(2) if a + b + c + d),
    key=lambda o: (-sum(min(v, 4 - v) for v in o[:3]), (o[0] * 7 + o[1] * 5 + o[2] * 3 + o[3]) % 11),
)


def send(src, dst, sems, device):
    return pltpu.make_async_remote_copy(
        src_ref=src,
        dst_ref=dst,
        send_sem=sems.at[0],
        recv_sem=sems.at[1],
        device_id=device,
        device_id_type=pl.DeviceIdType.MESH,
    )


def device_of(offset):
    g, w = lax.axis_index("grp"), lax.axis_index("wide")
    x = lax.rem(g + offset[0], 4)
    y = lax.rem(w // 8 + offset[1], 4)
    z = lax.rem(lax.rem(w // 2, 4) + offset[2], 4)
    c = lax.rem(lax.rem(w, 2) + offset[3], 2)
    return x, (y * 4 + z) * 2 + c


def lane():
    return lax.broadcasted_iota(jnp.int32, (8, 128), 1)


def sub():
    return lax.broadcasted_iota(jnp.int32, (8, 128), 0)


def rot(v, shift):
    return pltpu.roll(v, shift % 128, 1)


def turn(v, shift):
    return pltpu.roll(v, shift % 8, 0)


def potential(density):
    return 1.0 - jnp.exp(-density)


def moments(state):
    density = state[0]
    momentum = [None, None, None]
    for d in range(1, 19):
        density = density + state[d]
        for a in range(3):
            c = VELOCITIES[d][a]
            if c:
                m = momentum[a]
                momentum[a] = c * state[d] if m is None else (m + state[d] if c > 0 else m - state[d])
    return [density] + momentum


def relax(density, velocity, states, keep, gain):
    base = 1.0 - 1.5 * (velocity[0] * velocity[0] + velocity[1] * velocity[1] + velocity[2] * velocity[2])
    scaled = {w: (gain * w) * density for w in set(WEIGHTS[d] for d, _ in states)}
    entries = []
    for d, h in states:
        along = None
        for a in range(3):
            c = VELOCITIES[d][a]
            if c:
                term = velocity[a] if c > 0 else -velocity[a]
                along = term if along is None else along + term
        shape = base if along is None else base + along * (3.0 + 4.5 * along)
        entries.append(keep * h + scaled[WEIGHTS[d]] * shape)
    return entries


def collide(mom, pot, grad, states, tau, flip=None):
    inverse = 1.0 / mom[0]
    push = (-tau * COUPLING) * pot
    velocity = [(mom[1 + a] + push * grad[a]) * inverse for a in range(3)]
    if flip is not None:
        velocity[0] = velocity[0] * flip
    return relax(mom[0], velocity, states, 1.0 - 1.0 / tau, 1.0 / tau)


def fine_y(tiles, step, ghost):
    e = lane() & 15
    out = [None] * 8
    edge, inner, outer = (15, 0, 1) if step > 0 else (0, 1, 0)
    for r in range(4):
        across = rot(tiles[outer * 4 + r], 15 * step)
        out[inner * 4 + r] = jnp.where(e == edge, across, rot(tiles[inner * 4 + r], -step))
        out[outer * 4 + r] = jnp.where(e == edge, ghost[r], rot(tiles[outer * 4 + r], -step))
    return out


def fine_z(tiles, step):
    c = lane() >> 4
    moved = [rot(t, -16 * step) for t in tiles]
    edge = 7 if step > 0 else 0
    return [jnp.where(c == edge, moved[j ^ 1], moved[j]) for j in range(len(tiles))]


def fine_x(tiles, step, rows):
    s = sub()
    out = [None] * 8
    for k in range(2):
        for h in range(2):
            low, high = k * 4 + h, k * 4 + 2 + h
            if step > 0:
                out[low] = tiles[high]
                out[high] = jnp.where(s == 7, rows(4 + k * 2 + h), turn(tiles[low], -1))
            else:
                out[high] = tiles[low]
                out[low] = jnp.where(s == 0, rows(k * 2 + h), turn(tiles[high], 1))
    return out


def side_y(tile, step, ghost):
    e, k = lane() & 15, (sub() >> 1) & 1
    edge, inner = (15, 0) if step > 0 else (0, 1)
    across = turn(rot(tile, 15 * step), -2 * step)
    return jnp.where(e == edge, jnp.where(k == inner, across, ghost), rot(tile, -step))


def side_z(tile, step):
    c, h = lane() >> 4, sub() & 1
    moved = rot(tile, -16 * step)
    other = jnp.where(h == 0, turn(moved, -1), turn(moved, 1))
    return jnp.where(c == (7 if step > 0 else 0), other, moved)


def stencil(pot, up, down, back, front):
    total = pot * (1.0 / 18.0) + (up + down + back + front) * (1.0 / 36.0)
    return total, up - down, back - front


def rowcast(row):
    return jnp.broadcast_to(row, (8, 128))


def fine_step(state, mom, ghost_pot, ghost_post, ghost_side, halo, put, work):
    post, tee, face, rows = work
    pots = [mom[4, j] for j in range(8)]
    gp = [ghost_pot[h] for h in range(2)] * 2
    gz = fine_z(gp, 1)
    gz = [a - b for a, b in zip(gz, fine_z(gp, -1))]
    up, down = fine_y(pots, 1, gp), fine_y(pots, -1, gp)
    back, front = fine_z(pots, 1), fine_z(pots, -1)
    parts = [stencil(*v) for v in zip(pots, up, down, back, front)]
    total, dy, dz = ([p[i] for p in parts] for i in range(3))
    zz = [a + b for a, b in zip(fine_z(dy, 1), fine_z(dy, -1))]
    yy = [a + b for a, b in zip(fine_y(dz, 1, gz), fine_y(dz, -1, gz))]
    for j in range(8):
        tee[0, j] = total[j]
        tee[1, j] = dy[j] * (1.0 / 18.0) + zz[j] * (1.0 / 36.0)
        tee[2, j] = dz[j] * (1.0 / 18.0) + yy[j] * (1.0 / 36.0)
        tee[3, j] = dy[j]
        tee[4, j] = dz[j]

    def finish():
        flip = jnp.where(sub() < 4, 1.0, -1.0)
        near, far, own = potential(halo[0]), halo[9], face[...]
        outer, inner = ghost_side[0], ghost_side[1]

        def terms(tile, ghost):
            return stencil(tile, side_y(tile, 1, ghost), side_y(tile, -1, ghost), side_z(tile, 1), side_z(tile, -1))

        t1, y1, z1 = terms(near, outer)
        t2, y2, z2 = terms(far, outer)
        t0, y0, z0 = terms(own, inner)
        goz = side_z(outer, 1) - side_z(outer, -1)
        grad = [
            (t0 - t2) * flip,
            y1 * (1.0 / 18.0) + (y0 + y2 + side_z(y1, 1) + side_z(y1, -1)) * (1.0 / 36.0),
            z1 * (1.0 / 18.0) + (z0 + z2 + side_y(z1, 1, goz) + side_y(z1, -1, goz)) * (1.0 / 36.0),
        ]
        states = [(d, halo[4 + q]) for q, d in enumerate(X_PLUS)]
        for q, v in enumerate(collide([halo[i] for i in range(4)], near, grad, states, FINE_TAU, flip)):
            rows[q] = v
        rows[5], rows[6], rows[7] = t1, y1, z1

        def row(i):
            return lambda r: rowcast(rows[i, r : r + 1, :])

        total, dy, dz = ([tee[i, j] for j in range(8)] for i in (0, 3, 4))
        gx = [a - b for a, b in zip(fine_x(total, 1, row(5)), fine_x(total, -1, row(5)))]
        xy = [a + b for a, b in zip(fine_x(dy, 1, row(6)), fine_x(dy, -1, row(6)))]
        xz = [a + b for a, b in zip(fine_x(dz, 1, row(7)), fine_x(dz, -1, row(7)))]
        for j in range(8):
            tee[0, j] = gx[j]
            tee[1, j] = tee[1, j] + xy[j] * (1.0 / 36.0)
            tee[2, j] = tee[2, j] + xz[j] * (1.0 / 36.0)

        def body(j, _):
            values = collide(
                [mom[i, j] for i in range(4)],
                mom[4, j],
                [tee[i, j] for i in range(3)],
                [(d, state[d, j]) for d in range(19)],
                FINE_TAU,
            )
            for d in range(19):
                post[d, j] = values[d]
            return 0

        lax.fori_loop(0, 8, body, 0)
        for d in range(19):
            tiles = [post[d, j] for j in range(8)]
            cx, cy, cz = VELOCITIES[d]
            if cx:
                tiles = fine_x(tiles, -cx, row((X_PLUS if cx > 0 else X_MINUS).index(d)))
            if cz:
                tiles = fine_z(tiles, -cz)
            if cy:
                q = (Y_PLUS if cy > 0 else Y_MINUS).index(d)
                tiles = fine_y(tiles, -cy, [ghost_post[q, r] for r in range(4)])
            put(d, tiles)

    return finish


def fine_moments(state, mom):
    def body(j, _):
        values = moments([state[d, j] for d in range(19)])
        for i in range(4):
            mom[i, j] = values[i]
        mom[4, j] = potential(values[0])
        return 0

    lax.fori_loop(0, 8, body, 0)


def fine_faces(state, mom, out, face):
    for k in range(2):
        for h in range(2):
            r, low, high = k * 2 + h, k * 4 + h, k * 4 + 2 + h
            for i in range(4):
                out[i, r : r + 1, :] = mom[i, high, 7:8, :]
                out[i, 4 + r : 5 + r, :] = mom[i, low, 0:1, :]
            for q in range(5):
                out[4 + q, r : r + 1, :] = state[X_PLUS[q], high, 7:8, :]
                out[4 + q, 4 + r : 5 + r, :] = state[X_MINUS[q], low, 0:1, :]
            out[9, r : r + 1, :] = mom[4, low, 7:8, :]
            out[9, 4 + r : 5 + r, :] = mom[4, high, 0:1, :]
            face[r : r + 1, :] = mom[4, low, 0:1, :]
            face[4 + r : 5 + r, :] = mom[4, high, 7:8, :]


def kernel(
    fine_hbm, coarse_hbm, slots_hbm, fine_out, coarse_out,
    fine, coarse, slots, si, p1, r1_0, r1_1, r1_2, p2, r2, inv_v, inv_s,
    state, post, mom, tee, face, rows, out1, out2, halo1, halo2,
    layers, low_out, low_in, ghost, edge_r, edge_l, edge_in, ghost_post, ghost_side,
    cmom, face_c, halo_c, rest, rest_out, rest_in, ghost_t, ctee, cpost, cgrad, cedge,
    s1, s2, s3, sg, se, sc, sh1, sh2, sr,
):
    g, w = lax.axis_index("grp"), lax.axis_index("wide")
    me = g * 32 + w
    right, left = lax.rem(g + 1, 4), lax.rem(g + 3, 4)
    ahead, behind = lax.rem(w + 1, 32), lax.rem(w + 31, 32)
    barrier = pltpu.get_barrier_semaphore()
    r1 = (r1_0, r1_1, r1_2)
    loads = [pltpu.make_async_copy(*pair, si.at[i]) for i, pair in enumerate(((fine_hbm, fine), (slots_hbm, slots), (coarse_hbm, coarse)))]
    for load in loads:
        load.start()
    for offset in OFFSETS:
        pl.semaphore_signal(barrier, inc=1, device_id=device_of(offset), device_id_type=pl.DeviceIdType.MESH)

    for load in loads:
        load.wait()

    def pack(t, _):
        for k in range(2):
            for q in range(4):
                n = min(5, 19 - 5 * q)
                p1[k, t * 4 + q, 0:n, :] = fine[pl.ds(5 * q * 64 + t * 2 + k, n, stride=64), :]
        return 0

    lax.fori_loop(0, 32, pack, 0)

    place = sub() * 128 + lane()

    def invert(b, acc):
        return jnp.where(place == slots[b], b, acc)

    inv_v[...] = lax.fori_loop(0, 256, invert, jnp.zeros((8, 128), jnp.int32), unroll=8)
    fetch = pltpu.make_async_copy(inv_v, inv_s, s3)
    fetch.start()
    for k in range(2):
        for part, (lo, hi) in enumerate(PARTS):
            r1[part][2 * me + k, lo:hi, :] = p1[k, me, lo:hi, :]

    def coarse_body(i, _):
        values = moments([coarse[d, i] for d in range(19)])
        for a in range(4):
            cmom[a, i + 2] = values[a]
        cmom[4, i + 2] = potential(values[0])
        return 0

    lax.fori_loop(0, 8, coarse_body, 0)
    for q in range(5):
        face_c[0, q] = coarse[X_PLUS[q], 7]
        face_c[1, q] = coarse[X_MINUS[q], 0]
    for a in range(4):
        face_c[0, 5 + a] = cmom[a, 9]
        face_c[1, 5 + a] = cmom[a, 2]
    face_c[0, 9] = cmom[4, 8]
    face_c[1, 9] = cmom[4, 3]

    flat = coarse.reshape(19 * 64, 128)
    e, c_l, s = lane() & 15, lane() >> 4, sub()

    def layer_body(d, _):
        for h in range(2):
            v = None
            for m in range(4):
                t = rot(flat[pl.ds(d * 64 + h * 4 + m, 8, stride=8), :], 32 * m + 15)
                v = t if v is None else jnp.where(c_l >= 2 * m, t, v)
            layers[d, h] = v
        return 0

    lax.fori_loop(0, 19, layer_body, 0)

    def rescaled(source, is_low, factor, h):
        m = moments([source[d, h] for d in range(19)])
        inverse = 1.0 / m[0]
        u = [m[1] * inverse, m[2] * inverse * jnp.where(is_low, 1.0, -1.0), m[3] * inverse]
        states = [(d, jnp.where(is_low, source[d, h], source[Y_MINUS[q], h])) for q, d in enumerate(Y_PLUS)]
        return relax(m[0], u, states, factor, 1.0 - factor) + [potential(m[0])]

    for h in range(2):
        for q, v in enumerate(rescaled(layers, e == 14, TO_FINE, h)):
            low_out[q, h] = jnp.where((c_l & 1) == 1, rot(v, 16), v)

    pl.semaphore_wait(barrier, len(OFFSETS))
    to_ahead = send(low_out, low_in, sg, (g, ahead))
    to_ahead.start()
    for part, (lo, hi) in enumerate(PARTS):
        for offset in OFFSETS:
            x, y = device_of(offset)
            send(p1.at[:, x * 32 + y, lo:hi, :], r1[part].at[pl.ds(2 * me, 2), lo:hi, :], s1.at[part], (x, y)).start()
    cf_r = send(face_c.at[0], halo_c.at[0], sc.at[0], (right, w))
    cf_l = send(face_c.at[1], halo_c.at[1], sc.at[1], (left, w))
    cf_r.start()
    cf_l.start()

    to_ahead.wait_recv()
    for q in range(6):
        for h in range(2):
            v = jnp.where(e == 0, rot(low_in[q, h], -14), low_out[q, h])
            ghost[q, h] = v
            edge_r[q * 2 + h : q * 2 + h + 1, :] = v[7:8]
            edge_l[q * 2 + h : q * 2 + h + 1, :] = v[0:1]
    ge_r = send(edge_r, edge_in.at[0], se.at[0], (right, w))
    ge_l = send(edge_l, edge_in.at[1], se.at[1], (left, w))
    ge_r.start()
    ge_l.start()

    fetch.wait()

    everyone = [(0, 0, 0, 0)] + OFFSETS
    for part, (lo, hi) in enumerate(PARTS):
        arrived = r1[part].at[0:254, lo:hi, :]
        pltpu.make_async_copy(arrived, arrived, s1.at[part, 1]).wait()
        for start in range(0, 128, 8):
            group = everyone[start : start + 8]
            targets = [device_of(offset) for offset in group]
            owners = [x * 32 + y for x, y in targets]
            found = [[inv_s[m // 64, 2 * lax.rem(m, 64) + k] for k in range(2)] for m in owners]
            pieces = [[r1[part][b, lo:hi, :] for b in pair] for pair in found]
            for m, pair in zip(owners, pieces):
                for k in range(2):
                    p2[k, m, lo:hi, :] = pair[k]
            for m, pair, offset, device in zip(owners, pieces, group, targets):
                if any(offset):
                    send(p2.at[:, m, lo:hi, :], r2.at[:, me, lo:hi, :], s2.at[part], device).start()
                else:
                    for k in range(2):
                        r2[k, me, lo:hi, :] = pair[k]

    ge_r.wait_recv()
    ge_l.wait_recv()
    for q in range(5):
        v = [ghost[q, h] for h in range(2)]
        cx, _, cz = VELOCITIES[Y_PLUS[q]]
        if cz:
            v = fine_z(v, -cz)
        for h in range(2):
            low = high = v[h]
            if cx > 0:
                low = jnp.where(s == 0, rowcast(edge_in[0, q * 2 + h : q * 2 + h + 1, :]), turn(v[h], 1))
            if cx < 0:
                high = jnp.where(s == 7, rowcast(edge_in[1, q * 2 + h : q * 2 + h + 1, :]), turn(v[h], -1))
            ghost_post[q, h] = low
            ghost_post[q, 2 + h] = high
    for k in range(2):
        for h in range(2):
            r = k * 2 + h
            ghost_side[0, r : r + 1, :] = edge_in[0, 10 + h : 11 + h, :]
            ghost_side[0, 4 + r : 5 + r, :] = edge_in[1, 10 + h : 11 + h, :]
            ghost_side[1, r : r + 1, :] = ghost[5, h, 0:1, :]
            ghost_side[1, 4 + r : 5 + r, :] = ghost[5, h, 7:8, :]
    cf_r.wait_recv()
    cf_l.wait_recv()
    for side, (near, far) in enumerate(((1, 0), (10, 11))):
        for a in range(4):
            cmom[a, near] = halo_c[side, 5 + a]
        cmom[4, near] = potential(halo_c[side, 5])
        cmom[4, far] = halo_c[side, 9]

    def coarse_y(v, step):
        return jnp.where(lane() == (127 if step > 0 else 0), 0.0, rot(v, -step))

    def terms_body(i, _):
        v = cmom[4, i]
        t, dy, dz = stencil(v, coarse_y(v, 1), coarse_y(v, -1), turn(v, -1), turn(v, 1))
        ctee[0, i], ctee[1, i], ctee[2, i] = t, dy, dz
        return 0

    lax.fori_loop(0, 12, terms_body, 0)

    def coarse_post(i, states):
        dy, dz = ctee[1, i], ctee[2, i]
        grad = [
            ctee[0, i + 1] - ctee[0, i - 1],
            dy * (1.0 / 18.0) + (ctee[1, i + 1] + ctee[1, i - 1] + turn(dy, 1) + turn(dy, -1)) * (1.0 / 36.0),
            dz * (1.0 / 18.0) + (ctee[2, i + 1] + ctee[2, i - 1] + coarse_y(dz, 1) + coarse_y(dz, -1)) * (1.0 / 36.0),
        ]
        for a in range(3):
            cgrad[a, i] = grad[a]
        values = collide([cmom[a, i] for a in range(4)], cmom[4, i], grad, states, COARSE_TAU)
        for (d, _), v in zip(states, values):
            cpost[d, i] = v

    def post_body(i, _):
        coarse_post(i + 2, [(d, coarse[d, i]) for d in range(19)])
        return 0

    lax.fori_loop(0, 8, post_body, 0)
    coarse_post(1, [(d, halo_c[0, q]) for q, d in enumerate(X_PLUS)])
    coarse_post(10, [(d, halo_c[1, q]) for q, d in enumerate(X_MINUS)])

    def stream_body(i, _):
        for d in range(19):
            cx, cy, cz = VELOCITIES[d]
            v = cpost[d, i + 2 - cx]
            if cz:
                v = turn(v, cz)
            if cy:
                v = rot(v, cy)
            coarse_out[d, i] = v
        return 0

    lax.fori_loop(0, 8, stream_body, 0)

    def packed(load, count):
        v = None
        for i in count:
            t = rot(load(i), 2 * i + 1)
            v = t if v is None else jnp.where(lane() >= 2 * i, t, v)
        return v

    def edge_body(d, _):
        cedge[d] = packed(lambda i: coarse[d, i - 2], range(2, 10))
        return 0

    lax.fori_loop(0, 19, edge_body, 0)
    for side, (dirs, i) in enumerate(((X_PLUS, 1), (X_MINUS, 10))):
        for q, d in enumerate(dirs):
            cedge[d] = jnp.where((lane() >> 1) == i, rot(halo_c[side, q], 2 * i + 1), cedge[d])
    for a in range(5):
        cedge[19 + a] = packed(lambda i: cmom[a, i], range(1, 11))
    for a in range(3):
        cedge[24 + a] = packed(lambda i: cgrad[a, i], range(1, 11))

    for part, (lo, hi) in enumerate(PARTS):
        arrived = r2.at[:, 0:127, lo:hi, :]
        pltpu.make_async_copy(arrived, arrived, s2.at[part, 1]).wait()
    got = r2.reshape(2048, 128)
    for d in range(19):
        for k in range(2):
            for r in range(4):
                state[d, k * 4 + r] = got[pl.ds(((k * 128 + r * 4 + d // 5) * 8) + d % 5, 8, stride=128), :]

    fine_moments(state, mom)
    fine_faces(state, mom, out1, face)
    f1r = send(out1.at[:, 0:4], halo1.at[:, 0:4], sh1.at[0], (right, w))
    f1l = send(out1.at[:, 4:8], halo1.at[:, 4:8], sh1.at[1], (left, w))
    f1r.start()
    f1l.start()

    for d in range(19):
        for h in range(2):
            v = jnp.where(e < 8, state[d, h] + state[d, 2 + h], state[d, 4 + h] + state[d, 6 + h])
            v = v + rot(v, -1)
            rest[d, h] = 0.125 * (v + rot(v, -16))
    slot = lane() & 31
    for h in range(2):
        tile = jnp.zeros((8, 128), jnp.float32)
        for q, v in enumerate(rescaled(rest, e == 14, TO_COARSE, h)):
            tile = jnp.where(slot == 2 * q, rot(v, 2 * q), jnp.where(slot == 2 * q + 1, rot(v, 2 * q - 13), tile))
        rest_out[h] = tile
    rests = [
        send(rest_out, rest_in.at[i], sr.at[i], device)
        for i, device in enumerate(((g, behind), (right, w), (right, behind), (left, w), (left, behind)))
    ]
    for copy in rests:
        copy.start()

    work = (post, tee, face, rows)

    def keep(d, tiles):
        for j in range(8):
            state[d, j] = tiles[j]

    def give(d, tiles):
        for k in range(2):
            for r in range(4):
                fine_out[pl.ds(d * 64 + r * 2 + k, 8, stride=8), :] = tiles[k * 4 + r]

    ghost_pot = [ghost[5, h] for h in range(2)]
    finish = fine_step(state, mom, ghost_pot, ghost_post, ghost_side, halo1, keep, work)
    f1r.wait_recv()
    f1l.wait_recv()
    finish()
    fine_moments(state, mom)
    fine_faces(state, mom, out2, face)
    f2r = send(out2.at[:, 0:4], halo2.at[:, 0:4], sh2.at[0], (right, w))
    f2l = send(out2.at[:, 4:8], halo2.at[:, 4:8], sh2.at[1], (left, w))
    f2r.start()
    f2l.start()

    for copy in rests:
        copy.wait_recv()
    turned = ghost_t.reshape(192, 128)
    is_low = (lane() & 1) == 1
    for b, (low, high) in enumerate(((rest_out, rest_in.at[0]), (rest_in.at[1], rest_in.at[2]), (rest_in.at[3], rest_in.at[4]))):
        for h in range(2):
            v = jnp.where(is_low, low[h], high[h])
            for m in range(4):
                ghost_t[b, h * 4 + m] = rot(v, -32 * m)
    starts = [64 + 6, 64 + 7] + list(range(8)) + [128, 129]
    columns = [turned[pl.ds(r, 8, stride=8), :] for r in starts]
    entering = []
    for q in range(6):
        v = rot(columns[0], -2 * q)
        for i in range(1, 12):
            v = jnp.where(lane() >= 2 * i, rot(columns[i], 2 * i - 2 * q), v)
        entering.append(v)

    pg = entering[5]
    x_up, x_down, z_up, z_down = rot(pg, -2), rot(pg, 2), turn(pg, -1), turn(pg, 1)
    outward = pg * (1.0 / 18.0) + (x_up + x_down + z_up + z_down) * (1.0 / 36.0)
    grad = [
        cedge[24] + (x_up - x_down) * (1.0 / 36.0),
        cedge[25] + jnp.where(is_low, -outward, outward),
        cedge[26] + (z_up - z_down) * (1.0 / 36.0),
    ]
    again = collide(
        [cedge[19 + a] for a in range(4)], cedge[23], grad, [(d, cedge[d]) for d in range(19)], COARSE_TAU
    )
    for d in range(19):
        cx, cy, cz = VELOCITIES[d]
        v = again[d]
        if cy > 0:
            v, base, mask = jnp.where(is_low, v, rot(entering[Y_PLUS.index(d)], -1)), 0, lane() < 2
        elif cy < 0:
            v, base, mask = jnp.where(is_low, rot(entering[Y_MINUS.index(d)], 1), v), 126, lane() >= 126
        else:
            base, mask = 127, (lane() == 0) | (lane() == 127)
        if cz:
            v = turn(v, cz)
        for x in range(8):
            coarse_out[d, x] = jnp.where(mask, rot(v, base - 2 * (x + 2 - cx)), coarse_out[d, x])

    finish = fine_step(state, mom, ghost_pot, ghost_post, ghost_side, halo2, give, work)
    f2r.wait_recv()
    f2l.wait_recv()
    finish()
    for copy in (to_ahead, ge_r, ge_l, cf_r, cf_l, f1r, f1l, f2r, f2l, *rests):
        copy.wait_send()
    for part, (lo, hi) in enumerate(PARTS):
        for left_here, sems in ((r1[part].at[0:254, lo:hi, :], s1), (r2.at[:, 0:127, lo:hi, :], s2)):
            pltpu.make_async_copy(left_here, left_here, sems.at[part, 0]).wait()


def local(fine_pop, coarse_pop, new_slot):
    def tiles(*shape):
        return pltpu.VMEM(shape + (8, 128), jnp.float32)

    def sems(*shape):
        return pltpu.SemaphoreType.DMA(shape)

    vmem = pl.BlockSpec(memory_space=pltpu.VMEM)
    fine_out, coarse_out = pl.pallas_call(
        kernel,
        out_shape=(
            jax.ShapeDtypeStruct((1216, 128), jnp.float32),
            jax.ShapeDtypeStruct((19, 8, 8, 128), jnp.float32),
        ),
        in_specs=[pl.BlockSpec(memory_space=pltpu.HBM)] * 3,
        out_specs=(vmem, vmem),
        scratch_shapes=[
            pltpu.VMEM((1216, 128), jnp.float32), tiles(19, 8), pltpu.SMEM((256,), jnp.int32), sems(3),
            tiles(2, 128), tiles(256), tiles(256), tiles(256), tiles(2, 128), tiles(2, 128),
            pltpu.VMEM((8, 128), jnp.int32), pltpu.SMEM((8, 128), jnp.int32),
            tiles(19, 8), tiles(19, 8), tiles(5, 8), tiles(5, 8), tiles(), tiles(8),
            tiles(10), tiles(10), tiles(10), tiles(10),
            tiles(19, 2), tiles(6, 2), tiles(6, 2), tiles(6, 2),
            pltpu.VMEM((12, 128), jnp.float32), pltpu.VMEM((12, 128), jnp.float32),
            pltpu.VMEM((2, 12, 128), jnp.float32), tiles(5, 4), tiles(2),
            tiles(5, 12), tiles(2, 10), tiles(2, 10), tiles(19, 2), tiles(2), tiles(5, 2),
            tiles(3, 8), tiles(3, 12), tiles(19, 12), tiles(3, 12), tiles(27),
            sems(len(PARTS), 2), sems(len(PARTS), 2), pltpu.SemaphoreType.DMA, sems(2), sems(2, 2), sems(2, 2),
            sems(2, 2), sems(2, 2), sems(5, 2),
        ],
        compiler_params=pltpu.CompilerParams(
            collective_id=0, has_side_effects=True, vmem_limit_bytes=53836 * 1024
        ),
    )(fine_pop.reshape(2, 19, 32, 128).transpose(1, 2, 0, 3).reshape(1216, 128), coarse_pop, new_slot)
    fine_out = fine_out.reshape(19, 32, 2, 128).transpose(2, 0, 1, 3).reshape(2, 19, 4096)
    return fine_out, coarse_out


def solution(mesh):
    return jax.shard_map(
        local,
        mesh=mesh,
        in_specs=(P(("grp", "wide"), None, None), P(None, "grp", None, "wide"), P()),
        out_specs=(P(("grp", "wide"), None, None), P(None, "grp", None, "wide")),
        check_vma=False,
    )
```
